32 devices in a mesh: wide: 8 (over z, y), narrow: 4 (over x, core).
Axes of the slice: x: 2, y: 2, z: 4, core: 2. Of those that a mesh axis runs over, the one named last changes fastest.
Arguments:
- tokens: bfloat16 [16, 512, 768], P('wide', 'narrow'), may hold values from -6 to 6
- query_weight: bfloat16 [2, 768, 768], P(None, ('wide', 'narrow')), may hold values from -0.21875 to 0.21875
- key_weight: bfloat16 [2, 768, 768], P(None, ('wide', 'narrow')), may hold values from -0.21875 to 0.21875
- value_weight: bfloat16 [2, 768, 768], P(None, ('wide', 'narrow')), may hold values from -0.21875 to 0.21875
- out_weight: bfloat16 [2, 768, 768], P(None, ('wide', 'narrow')), may hold values from -0.875 to 0.875
- up_weight: bfloat16 [2, 768, 3072], P(None, ('wide', 'narrow')), may hold values from -0.21875 to 0.21875
- down_weight: bfloat16 [2, 3072, 768], P(None, ('wide', 'narrow')), may hold values from -0.109375 to 0.109375
- query_bias: bfloat16 [2, 768], P(None, ('wide', 'narrow')), may hold values from -1.796875 to 1.796875
- value_bias: bfloat16 [2, 768], P(None, ('wide', 'narrow')), may hold values from -1.796875 to 1.796875
- out_bias: bfloat16 [2, 768], P(None, ('wide', 'narrow')), may hold values from -1.796875 to 1.796875
- up_bias: bfloat16 [2, 3072], P(None, ('wide', 'narrow')), may hold values from -1.796875 to 1.796875
- down_bias: bfloat16 [2, 768], P(None, ('wide', 'narrow')), may hold values from -1.796875 to 1.796875
- first_gain: bfloat16 [2, 768], P(None, ('wide', 'narrow')), may hold values from 0.5 to 1.5
- first_shift: bfloat16 [2, 768], P(None, ('wide', 'narrow')), may hold values from -1.1953125 to 1.1953125
- second_gain: bfloat16 [2, 768], P(None, ('wide', 'narrow')), may hold values from 0.5 to 1.5
- second_shift: bfloat16 [2, 768], P(None, ('wide', 'narrow')), may hold values from -1.1953125 to 1.1953125
- lengths: int32 [16], P('wide'), may hold values from 1 to 512, as said below
- cotangent: bfloat16 [16, 512, 768], P('wide', 'narrow'), may hold values from -6 to 6
Outputs:
- output: bfloat16 [16, 512, 768], P('wide', 'narrow')
- tokens_grad: bfloat16 [16, 512, 768], P('wide', 'narrow')
- query_weight_grad: float32 [2, 768, 768], P(None, ('wide', 'narrow'))
- key_weight_grad: float32 [2, 768, 768], P(None, ('wide', 'narrow'))
- value_weight_grad: float32 [2, 768, 768], P(None, ('wide', 'narrow'))
- out_weight_grad: float32 [2, 768, 768], P(None, ('wide', 'narrow'))
- up_weight_grad: float32 [2, 768, 3072], P(None, ('wide', 'narrow'))
- down_weight_grad: float32 [2, 3072, 768], P(None, ('wide', 'narrow'))
- query_bias_grad: float32 [2, 768], P(None, ('wide', 'narrow'))
- value_bias_grad: float32 [2, 768], P(None, ('wide', 'narrow'))
- out_bias_grad: float32 [2, 768], P(None, ('wide', 'narrow'))
- up_bias_grad: float32 [2, 3072], P(None, ('wide', 'narrow'))
- down_bias_grad: float32 [2, 768], P(None, ('wide', 'narrow'))
- first_gain_grad: float32 [2, 768], P(None, ('wide', 'narrow'))
- first_shift_grad: float32 [2, 768], P(None, ('wide', 'narrow'))
- second_gain_grad: float32 [2, 768], P(None, ('wide', 'narrow'))
- second_shift_grad: float32 [2, 768], P(None, ('wide', 'narrow'))
The draws below stay inside these ranges and needn't reach their ends.
Inputs may be any that keep to these rules, and one draw needn't show every extreme that they name: `lengths`: in each aligned block of 2 pairs at least one pair has length 512; the others are heavy-tailed.
All inputs are finite; a program needn't handle non-finite values.
Results may differ from the reference program's by a relative error of at most 0.024.
Values may be sent and summed in bfloat16 or wider, within the bound.
No kernel may reach another device: no remote copies, remote signals or barrier semaphores. Data moves between devices by JAX's collectives and lax.ppermute only.
A program may use at most 192 MiB of HBM per device.

```python
import math
import jax
import jax.numpy as jnp
from jax import lax

D = 768
HEADS = 12
HD = 64
FF = 3072
SEQ = 512
LAYERS = 2
PAIRS_DEV = 2
PAIRS = 16


def draw_lengths(key, part):
    key = jax.random.fold_in(key, 11)
    key_octave, key_offset, key_choose = jax.random.split(key, 3)
    octave = jax.random.randint(key_octave, (PAIRS,), 0, 6)
    ceiling = jnp.maximum(jnp.right_shift(jnp.full((PAIRS,), SEQ, jnp.int32), octave), 1)
    halfway = ceiling // 2
    offset = jax.random.randint(key_offset, (PAIRS,), 0, ceiling - halfway)
    drawn = halfway + offset + 1
    chosen = jax.random.randint(key_choose, (PAIRS // PAIRS_DEV,), 0, PAIRS_DEV)
    position = jnp.arange(PAIRS)
    is_full = position % PAIRS_DEV == chosen[position // PAIRS_DEV]
    return jnp.where(is_full, SEQ, drawn).astype(jnp.int32)


def shard_levels(own_key, extent, cuts, low, largest):
    level = 1.0
    for dim, shards_of in cuts:
        draws = jax.random.uniform(jax.random.fold_in(jax.random.fold_in(own_key, 6), dim), (shards_of,), jnp.float32, low / len(cuts), largest / len(cuts))
        level = level * jnp.repeat(jnp.exp(draws), extent[dim] // shards_of).reshape((-1,) + (1,) * (len(extent) - 1 - dim))
    return level


def scatter_about(key, extent, scale, bound, cuts=(), kind=jnp.bfloat16):
    values = scale * jax.random.normal(key, extent, jnp.float32)
    if cuts:
        values = values * shard_levels(key, extent, cuts, -0.22, 0.18)
    return jnp.clip(values, -bound, bound).astype(kind)


def setup_inputs(seed: int = 0) -> dict:
    arg_keys = jax.random.split(jax.random.key(seed), 19)
    return {
        "tokens": scatter_about(arg_keys[0], (PAIRS, SEQ, D), 1.0, 6.0, ((0, 8), (1, 4))),
        "query_weight": scatter_about(arg_keys[1], (LAYERS, D, D), D ** -0.5, 0.21875, ((1, 32),)),
        "key_weight": scatter_about(arg_keys[2], (LAYERS, D, D), D ** -0.5, 0.21875, ((1, 32),)),
        "value_weight": scatter_about(arg_keys[3], (LAYERS, D, D), D ** -0.5, 0.21875, ((1, 32),)),
        "out_weight": scatter_about(arg_keys[4], (LAYERS, D, D), (D // 16) ** -0.5, 0.875, ((1, 32),)),
        "up_weight": scatter_about(arg_keys[5], (LAYERS, D, FF), D ** -0.5, 0.21875, ((1, 32),)),
        "down_weight": scatter_about(arg_keys[6], (LAYERS, FF, D), FF ** -0.5, 0.109375, ((1, 32),)),
        "query_bias": scatter_about(arg_keys[7], (LAYERS, D), 0.3, 1.796875, ((1, 32),)),
        "value_bias": scatter_about(arg_keys[8], (LAYERS, D), 0.3, 1.796875, ((1, 32),)),
        "out_bias": scatter_about(arg_keys[9], (LAYERS, D), 0.3, 1.796875, ((1, 32),)),
        "up_bias": scatter_about(arg_keys[10], (LAYERS, FF), 0.3, 1.796875, ((1, 32),)),
        "down_bias": scatter_about(arg_keys[11], (LAYERS, D), 0.3, 1.796875, ((1, 32),)),
        "first_gain": jnp.clip(1.0 + 0.1 * jax.random.normal(arg_keys[12], (LAYERS, D), jnp.float32), 0.5, 1.5).astype(jnp.bfloat16),
        "first_shift": scatter_about(arg_keys[13], (LAYERS, D), 0.2, 1.1953125, ((1, 32),)),
        "second_gain": jnp.clip(1.0 + 0.1 * jax.random.normal(arg_keys[14], (LAYERS, D), jnp.float32), 0.5, 1.5).astype(jnp.bfloat16),
        "second_shift": scatter_about(arg_keys[15], (LAYERS, D), 0.2, 1.1953125, ((1, 32),)),
        "lengths": draw_lengths(jax.random.fold_in(arg_keys[18], 71), 0),
        "cotangent": scatter_about(arg_keys[17], (PAIRS, SEQ, D), 1.0, 6.0, ((0, 8), (1, 4))),
    }


@jax.custom_vjp
def low(v):
    return lax.optimization_barrier(v.astype(jnp.bfloat16)).astype(jnp.float32)

@jax.custom_vjp
def low_back(v):
    return v

def low_keep(v):
    return (low(v), None)

def low_pass(kept, grad):
    return (grad,)

def back_keep(v):
    return (v, None)

def back_low(kept, grad):
    return (low(grad),)
low.defvjp(low_keep, low_pass)
low_back.defvjp(back_keep, back_low)
exact_mode = lax.Precision.HIGHEST

def layer_norm(values, gain, offset):
    average = lax.optimization_barrier(jnp.mean(values, axis=-1, keepdims=True))
    centred = values - average
    variance = lax.optimization_barrier(jnp.mean(centred * centred, axis=-1, keepdims=True))
    return centred * lax.rsqrt(variance + 1e-05) * gain + offset

def attend(inputs):
    queries, keys, values, valid = inputs
    scores = low_back(jnp.einsum('qhd,khd->hqk', queries, keys, precision=exact_mode) * HD ** (-0.5))
    scores = jnp.where(valid[None, None, :], scores, -1e+30)
    row_peak = lax.optimization_barrier(jnp.max(scores, axis=-1, keepdims=True))
    raised = jnp.exp(scores - row_peak)
    probs = raised / lax.optimization_barrier(jnp.sum(raised, axis=-1, keepdims=True))
    return jnp.einsum('hqk,khd->qhd', low(probs), values, precision=exact_mode)

def layer(hidden, params, valid):
    query_weight, key_weight, value_weight, out_weight, up_weight, down_weight, query_bias, value_bias, out_bias, up_bias, down_bias, first_gain, first_shift, second_gain, second_shift = params
    pairs_now = hidden.shape[0]
    flat = hidden.reshape(-1, D)
    inputs = low(flat)
    queries = low_back(low(jnp.dot(inputs, query_weight, precision=exact_mode) + query_bias))
    keys = low_back(low(jnp.dot(inputs, key_weight, precision=exact_mode)))
    values = low_back(low(jnp.dot(inputs, value_weight, precision=exact_mode) + value_bias))
    head_shape = (pairs_now, SEQ, HEADS, HD)
    mixed = lax.map(jax.checkpoint(attend), (queries.reshape(head_shape), keys.reshape(head_shape), values.reshape(head_shape), valid))
    mixed = low_back(low(mixed.reshape(-1, D)))
    branch = low_back(jnp.dot(mixed, out_weight, precision=exact_mode) + out_bias)
    normed = layer_norm(flat + branch, first_gain, first_shift)
    upward = low_back(jnp.dot(low(normed), up_weight, precision=exact_mode) + up_bias)
    activated = low(jax.nn.gelu(upward, approximate=False))
    downward = low_back(jnp.dot(activated, down_weight, precision=exact_mode) + down_bias)
    return layer_norm(normed + downward, second_gain, second_shift).reshape(hidden.shape)

def reference(tokens, query_weight, key_weight, value_weight, out_weight, up_weight, down_weight, query_bias, value_bias, out_bias, up_bias, down_bias, first_gain, first_shift, second_gain, second_shift, lengths, cotangent):
    params = tuple((piece.astype(jnp.float32) for piece in (query_weight, key_weight, value_weight, out_weight, up_weight, down_weight, query_bias, value_bias, out_bias, up_bias, down_bias, first_gain, first_shift, second_gain, second_shift)))
    group = math.gcd(PAIRS, 8)
    blocks = PAIRS // group
    valid_all = (jnp.arange(SEQ)[None, :] < lengths[:, None]).reshape(blocks, group, SEQ)
    hidden_all = tokens.astype(jnp.float32).reshape(blocks, group, SEQ, D)
    upstream_all = cotangent.astype(jnp.float32).reshape(blocks, group, SEQ, D)

    def run(carry, inputs):
        hidden, valid, upstream = inputs

        def forward(start, weights):
            current = start
            for index in range(LAYERS):
                current = layer(current, tuple((piece[index] for piece in weights)), valid)
            return current
        result, pullback = jax.vjp(forward, hidden, params)
        d_hidden, d_params = pullback(upstream)
        carry = tuple((total + part for total, part in zip(carry, d_params)))
        return (carry, (result.astype(jnp.bfloat16), d_hidden.astype(jnp.bfloat16)))
    zeros = tuple((jnp.zeros(piece.shape, jnp.float32) for piece in params))
    grads, (outputs, backs) = lax.scan(run, zeros, (hidden_all, valid_all, upstream_all))
    output = outputs.reshape(PAIRS, SEQ, D)
    tokens_grad = backs.reshape(PAIRS, SEQ, D)
    return (output, tokens_grad, grads[0], grads[1], grads[2], grads[3], grads[4], grads[5], grads[6], grads[7], grads[8], grads[9], grads[10], grads[11], grads[12], grads[13], grads[14])
```

```python
import functools

import jax
import jax.numpy as jnp
from jax import lax
from jax.experimental import pallas as pl
from jax.experimental.pallas import tpu as pltpu
from jax.sharding import PartitionSpec as P

D = 768
HEADS = 12
HD = 64
FF = 3072
LAYERS = 2
PAD = 128
LOW = jnp.bfloat16
FULL = jnp.float32


def bits_of(name):
    return lax.axis_size(name).bit_length() - 1


def swap(value, name, bit):
    pairs = [(i, i ^ (1 << bit)) for i in range(lax.axis_size(name))]
    return lax.ppermute(value, name, pairs)


def own_bit(name, bit):
    return (lax.axis_index(name) >> bit) & 1


def axis_of(name, bit):
    if name == "wide":
        return bits_of("wide") - 1 - bit
    return bits_of("wide") + bits_of("narrow") - 1 - bit


def order(first):
    far = [("wide", bit) for bit in range(bits_of("wide") - 1, 0, -1)]
    middle = [("wide", 0), ("narrow", 1)]
    if first == "narrow":
        middle.reverse()
    return far + middle + [("narrow", 0)]


def gather(shard, first):
    lead = bits_of("wide") + bits_of("narrow")
    held = shard.reshape((1,) * lead + shard.shape)
    for name, bit in order(first):
        other = swap(held, name, bit)
        mine_low = own_bit(name, bit) == 0
        held = jnp.concatenate(
            [jnp.where(mine_low, held, other), jnp.where(mine_low, other, held)],
            axis=axis_of(name, bit),
        )
    return held.reshape(-1, shard.shape[-1])


def scatter(whole, first):
    lead = bits_of("wide") + bits_of("narrow")
    count = lax.axis_size("wide") * lax.axis_size("narrow")
    held = whole.reshape((2,) * lead + (whole.shape[0] // count, whole.shape[1]))
    for name, bit in reversed(order(first)):
        axis = axis_of(name, bit)
        mine = own_bit(name, bit)
        kept = lax.dynamic_index_in_dim(held, mine, axis)
        other = swap(lax.dynamic_index_in_dim(held, 1 - mine, axis), name, bit)
        total = kept.astype(FULL) + other.astype(FULL)
        held = total.astype(LOW)
    return total.reshape(total.shape[-2:])


def stack_heads(pair):
    lane = lax.broadcasted_iota(jnp.int32, pair.shape, 1)
    zero = jnp.zeros_like(pair)
    return jnp.concatenate(
        [jnp.where(lane < HD, pair, zero), jnp.where(lane < HD, zero, pair)], axis=0
    )


def pick_heads(stacked):
    rows = stacked.shape[0] // 2
    lane = lax.broadcasted_iota(jnp.int32, (rows, stacked.shape[1]), 1)
    return jnp.where(lane < HD, stacked[:rows], stacked[rows:])


def dot_t(left, right):
    return lax.dot_general(left, right, (((1,), (1,)), ((), ())), preferred_element_type=FULL)


def dot_l(left, right):
    return lax.dot_general(left, right, (((0,), (0,)), ((), ())), preferred_element_type=FULL)


def attend_kernel(meta, query, *rest):
    count = (len(rest) - 2) // 2
    keys, values, mixed, probs = rest[:count], rest[count : 2 * count], rest[-2], rest[-1]
    length = meta[pl.program_id(0)]
    pairs = pl.num_programs(0)
    stacked = stack_heads(query[0])
    parts = []
    for j in range(count):
        part = dot_t(stacked, keys[j][0]) * HD**-0.5
        place = meta[pairs + j] + lax.broadcasted_iota(jnp.int32, part.shape, 1)
        parts.append(jnp.where(place < length, part, -1e30))
    scores = jnp.concatenate(parts, axis=1)
    raised = jnp.exp(scores - jnp.max(scores, axis=1, keepdims=True))
    low = (raised / jnp.sum(raised, axis=1, keepdims=True)).astype(LOW)
    probs[0, 0] = low
    value = jnp.concatenate([block[0] for block in values], axis=0)
    mixed[0] = pick_heads(jnp.dot(low, value, preferred_element_type=FULL)).astype(LOW)


def attend(queries, blocks, meta):
    pairs, rows, width = queries.shape
    steps = width // 128
    count = len(blocks)
    spec_key = pl.BlockSpec((1, rows, 128), lambda p, h, meta: (p, 0, h))
    spec_value = pl.BlockSpec((1, rows, 128), lambda p, h, meta: (p, 0, steps + h))
    return pl.pallas_call(
        attend_kernel,
        grid_spec=pltpu.PrefetchScalarGridSpec(
            num_scalar_prefetch=1,
            grid=(pairs, steps),
            in_specs=[spec_key] + [spec_key] * count + [spec_value] * count,
            out_specs=[
                spec_key,
                pl.BlockSpec((1, 1, 2 * rows, count * rows), lambda p, h, meta: (p, h, 0, 0)),
            ],
        ),
        out_shape=[
            jax.ShapeDtypeStruct(queries.shape, LOW),
            jax.ShapeDtypeStruct((pairs, steps, 2 * rows, count * rows), LOW),
        ],
    )(meta, queries, *blocks, *blocks)


def attend_back_kernel(count, query, mixed_grad, probs, *rest):
    keys, values = rest[:count], rest[count : 2 * count]
    query_grad, key_grad, value_grad = rest[2 * count :]
    rows = query.shape[1]
    queries = stack_heads(query[0])
    grads = stack_heads(mixed_grad[0])
    low = probs[0, 0]
    key = jnp.concatenate([block[0] for block in keys], axis=0)
    value = jnp.concatenate([block[0] for block in values], axis=0)
    prob_grad = dot_t(grads, value)
    wide = low.astype(FULL)
    weighted = jnp.sum(wide * prob_grad, axis=1, keepdims=True)
    score_grad = (wide * (prob_grad - weighted)).astype(LOW)
    query_grad[0] = (
        pick_heads(jnp.dot(score_grad, key, preferred_element_type=FULL)) * HD**-0.5
    ).astype(LOW)
    key_all = (dot_l(score_grad, queries) * HD**-0.5).astype(LOW)
    value_all = dot_l(low, grads).astype(LOW)
    for j in range(count):
        key_grad[j, 0] = key_all[j * rows : (j + 1) * rows]
        value_grad[j, 0] = value_all[j * rows : (j + 1) * rows]


def attend_back(queries, mixed_grad, probs, blocks):
    pairs, rows, width = queries.shape
    steps = width // 128
    count = len(blocks)
    spec_key = pl.BlockSpec((1, rows, 128), lambda p, h: (p, 0, h))
    spec_value = pl.BlockSpec((1, rows, 128), lambda p, h: (p, 0, steps + h))
    spec_probs = pl.BlockSpec((1, 1, 2 * rows, count * rows), lambda p, h: (p, h, 0, 0))
    spec_all = pl.BlockSpec((count, 1, rows, 128), lambda p, h: (0, p, 0, h))
    shape_all = jax.ShapeDtypeStruct((count, pairs, rows, width), LOW)
    return pl.pallas_call(
        functools.partial(attend_back_kernel, count),
        grid=(pairs, steps),
        in_specs=[spec_key, spec_key, spec_probs] + [spec_key] * count + [spec_value] * count,
        out_specs=[spec_key, spec_all, spec_all],
        out_shape=[jax.ShapeDtypeStruct(queries.shape, LOW), shape_all, shape_all],
    )(queries, mixed_grad, probs, *blocks, *blocks)


def matmul(left, right):
    return jnp.dot(left, right, preferred_element_type=FULL)


def normalise(values):
    average = jnp.mean(values, axis=-1, keepdims=True)
    centred = values - average
    variance = jnp.mean(centred * centred, axis=-1, keepdims=True)
    scale = lax.rsqrt(variance + 1e-05)
    return centred * scale, scale


def normalise_back(grad, gain, unit, scale):
    scaled = grad * gain
    first = jnp.mean(scaled, axis=-1, keepdims=True)
    second = jnp.mean(scaled * unit, axis=-1, keepdims=True)
    return scale * (scaled - first - unit * second)


def share_pair(block):
    held = [block]
    for bit in range(bits_of("narrow") - 1, -1, -1):
        stride = 1 << bit
        others = [swap(piece, "narrow", bit) for piece in held]
        held = [
            piece for both in zip(held, others) for piece in both
        ]
        del stride
    return held


def forward_layer(hidden, weights, vectors, meta, shape):
    pairs, rows_pair = shape
    attention, up, down = weights
    inputs = hidden.astype(LOW)
    both = matmul(inputs, attention[:, D : 3 * D])
    offset = jnp.concatenate([jnp.zeros((D,), LOW), vectors["value_bias"]])
    both = (both + offset).astype(LOW).reshape(pairs, rows_pair, 2 * D)
    blocks = share_pair(both)
    queries = (matmul(inputs, attention[:, :D]) + vectors["query_bias"]).astype(LOW)
    queries = queries.reshape(pairs, rows_pair, D)
    mixed, probs = attend(queries, blocks, meta)
    mixed = mixed.reshape(-1, D)
    pre_one = hidden + (matmul(mixed, attention[:, 3 * D : 4 * D]) + vectors["out_bias"])
    unit_one, scale_one = normalise(pre_one)
    normed = unit_one * vectors["first_gain"] + vectors["first_shift"]
    normed_low = normed.astype(LOW)
    upward = matmul(normed_low, up) + vectors["up_bias"]
    share = 0.5 * (1.0 + lax.erf(upward * (0.5**0.5)))
    density = jnp.exp(-0.5 * upward * upward) * 0.3989422804014327
    activated = (upward * share).astype(LOW)
    slope = (share + upward * density).astype(LOW)
    pre_two = normed + (matmul(activated, down) + vectors["down_bias"])
    unit_two, scale_two = normalise(pre_two)
    result = unit_two * vectors["second_gain"] + vectors["second_shift"]
    kept = (inputs, queries, blocks, probs, mixed, unit_one, scale_one, normed_low)
    kept += (activated, slope, unit_two, scale_two)
    return result, kept


def column_sum(values):
    return jnp.sum(values.astype(FULL), axis=0)


def left_t(left, right):
    return jnp.einsum("ra,rb->ab", left, right, preferred_element_type=FULL).astype(LOW)


def right_t(left, right):
    return jnp.einsum("ra,ba->rb", left, right, preferred_element_type=FULL)


def gather_sum(parts):
    held = list(parts)
    for bit in range(bits_of("narrow")):
        kept, sent = held[0::2], held[1::2]
        others = [swap(piece, "narrow", bit) for piece in sent]
        held = [
            (mine.astype(FULL) + other.astype(FULL)).astype(LOW)
            for mine, other in zip(kept, others)
        ]
    return held[0]


def backward_layer(upstream, kept, weights, vectors, shape):
    pairs, rows_pair = shape
    attention, up, down = weights
    (inputs, queries, blocks, probs, mixed, unit_one, scale_one, normed_low) = kept[:8]
    activated, slope, unit_two, scale_two = kept[8:]
    grads = {}
    grads["second_gain"] = column_sum(upstream * unit_two)
    grads["second_shift"] = column_sum(upstream)
    d_two = normalise_back(upstream, vectors["second_gain"], unit_two, scale_two)
    down_grad = d_two.astype(LOW)
    up_grad = (right_t(down_grad, down) * slope).astype(LOW)
    grads["down_bias"] = column_sum(down_grad)
    grads["up_bias"] = column_sum(up_grad)
    d_down = left_t(activated, down_grad)
    d_up = left_t(normed_low, up_grad)
    d_normed = d_two + right_t(up_grad, up)
    grads["first_gain"] = column_sum(d_normed * unit_one)
    grads["first_shift"] = column_sum(d_normed)
    d_one = normalise_back(d_normed, vectors["first_gain"], unit_one, scale_one)
    branch_grad = d_one.astype(LOW)
    grads["out_bias"] = column_sum(branch_grad)
    mixed_grad = right_t(branch_grad, attention[:, 3 * D : 4 * D]).astype(LOW)
    query_grad, key_parts, value_parts = attend_back(
        queries, mixed_grad.reshape(queries.shape), probs, blocks
    )
    count = len(blocks)
    both_parts = [
        jnp.stack([key_parts[j], value_parts[j]], axis=0) for j in range(count)
    ]
    both = gather_sum(both_parts)
    query_grad = query_grad.reshape(-1, D)
    key_grad, value_grad = both[0].reshape(-1, D), both[1].reshape(-1, D)
    grads["query_bias"] = column_sum(query_grad)
    grads["value_bias"] = column_sum(value_grad)
    three = jnp.concatenate([query_grad, key_grad, value_grad], axis=1)
    d_input = d_one + right_t(three, attention[:, : 3 * D])
    d_attention = jnp.concatenate([left_t(inputs, three), left_t(mixed, branch_grad)], axis=1)
    return d_input, (d_attention, d_up, d_down), grads


NAMES = (
    "query_bias",
    "value_bias",
    "out_bias",
    "down_bias",
    "first_gain",
    "first_shift",
    "second_gain",
    "second_shift",
    "up_bias",
)
COLUMNS = 8 + FF // D


def pack_shards(shards):
    rows = []
    for layer in shards:
        for name in NAMES:
            piece = layer[name]
            rows.append(piece.reshape(-1, layer[NAMES[0]].shape[0]))
    stacked = jnp.concatenate(rows, axis=0)
    stacked = jnp.pad(stacked, ((0, PAD - stacked.shape[0]), (0, 0)))
    return stacked.T


def unpack_whole(columns):
    count = lax.axis_size("wide") * lax.axis_size("narrow")
    rows = columns.T
    out = []
    for index in range(LAYERS):
        base = index * COLUMNS
        vectors = {name: rows[base + i] for i, name in enumerate(NAMES[:-1])}
        up = rows[base + 8 : base + COLUMNS].reshape(FF // D, count, D // count)
        vectors["up_bias"] = up.transpose(1, 0, 2).reshape(FF)
        out.append(vectors)
    return out


def pack_whole(grads):
    count = lax.axis_size("wide") * lax.axis_size("narrow")
    rows = []
    for layer in grads:
        rows += [layer[name].reshape(1, D) for name in NAMES[:-1]]
        up = layer["up_bias"].reshape(count, FF // D, D // count)
        rows.append(up.transpose(1, 0, 2).reshape(FF // D, D))
    stacked = jnp.concatenate(rows, axis=0)
    stacked = jnp.pad(stacked, ((0, PAD - stacked.shape[0]), (0, 0)))
    return stacked.T.astype(LOW)


def unpack_shards(columns):
    rows = columns.T
    out = []
    for index in range(LAYERS):
        base = index * COLUMNS
        layer = {name: rows[base + i] for i, name in enumerate(NAMES[:-1])}
        layer["up_bias"] = rows[base + 8 : base + COLUMNS].reshape(-1)
        out.append(layer)
    return out


def body(
    tokens,
    query_weight,
    key_weight,
    value_weight,
    out_weight,
    up_weight,
    down_weight,
    query_bias,
    value_bias,
    out_bias,
    up_bias,
    down_bias,
    first_gain,
    first_shift,
    second_gain,
    second_shift,
    lengths,
    cotangent,
):
    pairs, rows_pair, width = tokens.shape
    shape = (pairs, rows_pair)
    given = dict(
        query_bias=query_bias,
        value_bias=value_bias,
        out_bias=out_bias,
        up_bias=up_bias,
        down_bias=down_bias,
        first_gain=first_gain,
        first_shift=first_shift,
        second_gain=second_gain,
        second_shift=second_shift,
    )
    shards = [{name: given[name][index] for name in NAMES} for index in range(LAYERS)]
    weights = []
    vectors = None
    for index in range(LAYERS):
        attention = [query_weight[index], key_weight[index], value_weight[index], out_weight[index]]
        if index == 0:
            attention.append(pack_shards(shards))
        attention = gather(jnp.concatenate(attention, axis=1), "wide")
        if index == 0:
            vectors = unpack_whole(attention[:, 4 * D :])
        up = gather(up_weight[index], "narrow")
        down = gather(down_weight[index], "wide")
        weights.append((attention, up, down))
    narrow = lax.axis_index("narrow")
    places = [(narrow ^ j) * rows_pair for j in range(lax.axis_size("narrow"))]
    meta = jnp.concatenate([lengths, jnp.stack(places).astype(jnp.int32)])
    hidden = tokens.astype(FULL).reshape(-1, width)
    kept = []
    for index in range(LAYERS):
        hidden, saved = forward_layer(hidden, weights[index], vectors[index], meta, shape)
        kept.append(saved)
    output = hidden.astype(LOW).reshape(tokens.shape)
    upstream = cotangent.astype(FULL).reshape(-1, width)
    small = [None] * LAYERS
    large = [None] * LAYERS
    for index in reversed(range(LAYERS)):
        upstream, large[index], small[index] = backward_layer(
            upstream, kept[index], weights[index], vectors[index], shape
        )
    tokens_grad = upstream.astype(LOW).reshape(tokens.shape)
    shares = [None] * LAYERS
    for index in reversed(range(LAYERS)):
        d_attention, d_up, d_down = large[index]
        if index == 0:
            d_attention = jnp.concatenate([d_attention, pack_whole(small)], axis=1)
        shares[index] = (
            scatter(d_attention, "wide"),
            scatter(d_up, "narrow"),
            scatter(d_down, "wide"),
        )
    vector_shares = unpack_shards(shares[0][0][:, 4 * D :])

    def stacked(select):
        return jnp.stack([select(index) for index in range(LAYERS)], axis=0)

    weight_grads = [
        stacked(lambda index, i=i: shares[index][0][:, i * D : (i + 1) * D]) for i in range(4)
    ]
    weight_grads.append(stacked(lambda index: shares[index][1]))
    weight_grads.append(stacked(lambda index: shares[index][2]))
    names = (
        "query_bias",
        "value_bias",
        "out_bias",
        "up_bias",
        "down_bias",
        "first_gain",
        "first_shift",
        "second_gain",
        "second_shift",
    )
    vector_grads = [stacked(lambda index, n=name: vector_shares[index][n]) for name in names]
    return (output, tokens_grad, *weight_grads, *vector_grads)


def solution(mesh):
    rows = P("wide", "narrow", None)
    weight = P(None, ("wide", "narrow"), None)
    vector = P(None, ("wide", "narrow"))
    return jax.shard_map(
        body,
        mesh=mesh,
        in_specs=(rows,) + (weight,) * 6 + (vector,) * 9 + (P("wide"), rows),
        out_specs=(rows, rows) + (weight,) * 6 + (vector,) * 9,
        check_vma=False,
    )
```

```python
import functools
import heapq

import jax
import jax.numpy as jnp
from jax import lax
from jax.experimental import pallas as pl
from jax.experimental.pallas import tpu as pltpu
import numpy as np
from jax.sharding import PartitionSpec as P

D = 768
HEADS = 12
HD = 64
FF = 3072
LAYERS = 2
PAD = 128
HALF = D // 2
LOW = jnp.bfloat16
FULL = jnp.float32


def bits_of(name):
    return lax.axis_size(name).bit_length() - 1


def swap(value, name, bit):
    pairs = [(i, i ^ (1 << bit)) for i in range(lax.axis_size(name))]
    return lax.ppermute(value, name, pairs)


def swap_core(value):
    return swap(value, "narrow", 0)


def own_bit(name, bit):
    return (lax.axis_index(name) >> bit) & 1


def core_low():
    return own_bit("narrow", 0) == 0


def axis_of(name, bit):
    if name == "wide":
        return bits_of("wide") - 1 - bit
    return bits_of("wide")


def order(first):
    far = [("wide", bit) for bit in range(bits_of("wide") - 1, 0, -1)]
    middle = [("wide", 0), ("narrow", 1)]
    if first == "narrow":
        middle.reverse()
    return far + middle


def flip(values):
    half = values.shape[-1] // 2
    turned = jnp.concatenate([values[..., half:], values[..., :half]], axis=-1)
    return jnp.where(core_low(), values, turned)


def link_of(name, bit):
    if name == "narrow":
        return "x"
    return "y" if bit == 0 else "z"


RATE = 40e3
BACK_RATE = 12e3
CORE_RATE = 500e3
COPY_RATE = 1.0e6
START = 1.5
STEP = 0.8


class Gather:
    def __init__(self, shard, first, rank):
        self.stages = order(first) + [("core", 0)]
        lead = bits_of("wide") + 1
        self.held = shard.reshape((1,) * lead + shard.shape)
        self.rank = rank
        self.done = False

    def link(self, k):
        name, bit = self.stages[k]
        return "core" if name == "core" else link_of(name, bit)

    def time(self, k):
        name, bit = self.stages[k]
        size = self.held.size * 2
        if name == "core":
            return size / CORE_RATE
        return size / RATE * (2 if name == "wide" and bit > 1 else 1)

    def operand(self, k):
        if self.stages[k][0] == "core":
            self.held = self.held.reshape(-1, self.held.shape[-1])
        return self.held

    def send(self, k, value):
        self.held = value
        name, bit = self.stages[k]
        return swap_core(value) if name == "core" else swap(value, name, bit)

    def finish(self, k, other):
        name, bit = self.stages[k]
        if name == "core":
            self.mine, self.other = self.held, other
            self.done = True
            return 0.0
        axis = axis_of(name, bit)
        shape = self.held.shape[:axis] + (2,) + self.held.shape[axis + 1 :]
        place = lax.broadcasted_iota(jnp.int32, shape, axis)
        self.held = jnp.where(place == own_bit(name, bit), self.held, other)
        return STEP + self.held.size * 4 / COPY_RATE


class Scatter:
    def __init__(self, sent, kept, first, rank, groups=1):
        self.groups = groups
        self.stages = [("core", 0)] + order(first)[::-1]
        self.sent, self.kept = sent, kept
        self.rank = rank
        self.done = False

    def link(self, k):
        name, bit = self.stages[k]
        return "core" if name == "core" else link_of(name, bit)

    def time(self, k):
        name, bit = self.stages[k]
        size = self.sent.size * 2
        if name == "core":
            return size / CORE_RATE
        return size / BACK_RATE * (2 if name == "wide" and bit > 1 else 1)

    def operand(self, k):
        return self.sent

    def send(self, k, value):
        name, bit = self.stages[k]
        return swap_core(value) if name == "core" else swap(value, name, bit)

    def finish(self, k, other):
        cost = 2 * STEP + other.size * 6 / COPY_RATE
        if k == 0:
            self.kept = self.kept()
            cost += STEP + other.size * 2 / COPY_RATE
            chips = lax.axis_size("wide") * lax.axis_size("narrow") // 2
            shape = (self.groups,) + (2,) * (bits_of("wide") + 1)
            shape += (other.shape[0] // (chips * self.groups), other.shape[1])
            self.kept, other = self.kept.reshape(shape), other.reshape(shape)
        if k + 1 == len(self.stages):
            total = self.kept.astype(FULL) + other.astype(FULL)
            self.result = total.astype(LOW).reshape(-1, *total.shape[-2:])
            self.done = True
            return cost
        name, bit = self.stages[k + 1]
        axis, mine = 1 + axis_of(name, bit), own_bit(name, bit)

        def part(which):
            cut = [lax.dynamic_index_in_dim(value, which, axis) for value in (self.kept, other)]
            return (cut[0].astype(FULL) + cut[1].astype(FULL)).astype(LOW)

        self.sent, self.kept = part(1 - mine), part(mine)
        return cost


class Exchange:
    def __init__(self, value, bit, rank):
        self.value, self.bit, self.rank = value, bit, rank
        self.done = False

    def link(self, k):
        return "core" if self.bit == 0 else "x"

    def time(self, k):
        return self.value.size * 2 / (CORE_RATE if self.bit == 0 else RATE)

    def operand(self, k):
        return self.value

    def send(self, k, value):
        self.value = value
        return swap(value, "narrow", self.bit)

    def finish(self, k, other):
        self.other = other
        self.done = True
        return 0.0


class Pump:
    def __init__(self, depth=2):
        self.now = 0.0
        self.depth = depth
        self.flying = []
        self.links = {}
        self.count = 0
        self.last = None
        self.sent = None
        self.value = None

    def add(self, stream):
        self.request(stream, 0)

    def request(self, stream, k):
        link = self.links.setdefault(stream.link(k), [0, 0.0, []])
        if link[0] < self.depth:
            self.issue(stream, k, link)
        else:
            self.count += 1
            heapq.heappush(link[2], (stream.rank, self.count, stream, k))

    def issue(self, stream, k, link):
        operand = stream.operand(k)
        for other in (self.last, self.sent):
            if other is not None:
                operand, _ = lax.optimization_barrier((operand, other))
        self.sent = operand
        if self.value is not None:
            operand, self.value = lax.optimization_barrier((operand, self.value))
        link[0] += 1
        self.now += 0.3 if stream.link(k) == "core" else START
        end = max(self.now, link[1]) + stream.time(k) + 0.7
        link[1] = end - 0.7
        other = stream.send(k, operand)
        if stream.link(k) == "core":
            self.sent = other
        self.count += 1
        heapq.heappush(self.flying, (end, self.count, stream, k, other))

    def step(self):
        end, _, stream, k, other = heapq.heappop(self.flying)
        self.now = max(self.now, end)
        link = self.links[stream.link(k)]
        link[0] -= 1
        self.last = other
        self.now += stream.finish(k, other)
        if not stream.done:
            self.request(stream, k + 1)
        if link[2] and link[0] < self.depth:
            _, _, waiting, j = heapq.heappop(link[2])
            self.issue(waiting, j, link)

    def advance(self, time, value):
        self.value = value
        self.now += time
        while self.flying and self.flying[0][0] <= self.now:
            self.step()
        value, self.value = self.value, None
        return value

    def idle(self, time):
        while self.flying and self.flying[0][0] <= time:
            self.step()
        self.now = max(self.now, time)

    def need(self, streams, value=None):
        self.value = value
        while not all(stream.done for stream in streams):
            self.step()
        value, self.value = self.value, None
        return value


BLOCKS = D // 128


def stack_heads(pair):
    lane = lax.broadcasted_iota(jnp.int32, pair.shape, 1)
    zero = jnp.zeros_like(pair)
    return jnp.concatenate(
        [jnp.where(lane < HD, pair, zero), jnp.where(lane < HD, zero, pair)], axis=0
    )


def pick_heads(stacked):
    rows = stacked.shape[0] // 2
    lane = lax.broadcasted_iota(jnp.int32, (rows, stacked.shape[1]), 1)
    return jnp.where(lane < HD, stacked[:rows], stacked[rows:])


def dot_t(left, right):
    return lax.dot_general(left, right, (((1,), (1,)), ((), ())), preferred_element_type=FULL)


def dot_l(left, right):
    return lax.dot_general(left, right, (((0,), (0,)), ((), ())), preferred_element_type=FULL)


def attend_kernel(meta, query, key_own, value_own, key_other, value_other, mixed, probs):
    length = meta[0]
    stacked = stack_heads(query[...])
    keys = jnp.concatenate([key_own[...], key_other[...]], axis=0)
    scores = dot_t(stacked, keys) * HD**-0.5
    rows = keys.shape[0] // 4
    column = lax.broadcasted_iota(jnp.int32, (1, keys.shape[0]), 1)
    place = column + meta[1]
    for j in range(1, 4):
        place = jnp.where(column >= j * rows, column - j * rows + meta[1 + j], place)
    scores = jnp.where(place < length, scores, -1e30)
    raised = jnp.exp(scores - jnp.max(scores, axis=1, keepdims=True))
    low = (raised / jnp.sum(raised, axis=1, keepdims=True)).astype(LOW)
    probs[0] = low
    values = jnp.concatenate([value_own[...], value_other[...]], axis=0)
    mixed[...] = pick_heads(jnp.dot(low, values, preferred_element_type=FULL)).astype(LOW)


def specs(rows):
    def at(index):
        return pl.BlockSpec((rows, 128), index)

    plain = at(lambda h, *_: (0, h))
    far = at(lambda h, *_: (0, BLOCKS + h))
    probs = pl.BlockSpec((1, 2 * rows, 2 * rows), lambda h, *_: (h, 0, 0))
    return plain, [plain, far, plain, far], probs


def attend(queries, own, other, meta):
    rows, width = queries.shape
    plain, keys, probs = specs(rows)
    return pl.pallas_call(
        attend_kernel,
        grid_spec=pltpu.PrefetchScalarGridSpec(
            num_scalar_prefetch=1,
            grid=(BLOCKS,),
            in_specs=[plain] + keys,
            out_specs=[plain, probs],
        ),
        out_shape=[
            jax.ShapeDtypeStruct(queries.shape, LOW),
            jax.ShapeDtypeStruct((BLOCKS, 2 * rows, 2 * rows), LOW),
        ],
        cost_estimate=pl.CostEstimate(
            flops=BLOCKS * 4 * rows * rows * 512 * 2,
            bytes_accessed=8 * rows * width * 2,
            transcendentals=BLOCKS * 4 * rows * rows,
        ),
    )(meta, queries, own, own, other, other)


def attend_back_kernel(
    query,
    key_own,
    value_own,
    key_other,
    value_other,
    mixed_grad,
    probs,
    query_grad,
    both_grad,
    both_grad_other,
):
    rows = query.shape[0]
    queries = stack_heads(query[...])
    grads = stack_heads(mixed_grad[...])
    low = probs[0]
    keys = jnp.concatenate([key_own[...], key_other[...]], axis=0)
    values = jnp.concatenate([value_own[...], value_other[...]], axis=0)
    prob_grad = dot_t(grads, values)
    wide = low.astype(FULL)
    weighted = jnp.sum(wide * prob_grad, axis=1, keepdims=True)
    score_grad = (wide * (prob_grad - weighted)).astype(LOW)
    query_grad[...] = (
        pick_heads(jnp.dot(score_grad, keys, preferred_element_type=FULL)) * HD**-0.5
    ).astype(LOW)
    key_all = (dot_l(score_grad, queries) * HD**-0.5).astype(LOW)
    value_all = dot_l(low, grads).astype(LOW)
    both_grad[0] = key_all[:rows]
    both_grad[1] = value_all[:rows]
    both_grad_other[0] = key_all[rows:]
    both_grad_other[1] = value_all[rows:]


def attend_back(queries, mixed_grad, probs, own, other):
    rows, width = queries.shape
    plain, keys, spec_probs = specs(rows)
    part = jax.ShapeDtypeStruct((2, rows, width), LOW)
    part_spec = pl.BlockSpec((2, rows, 128), lambda h: (0, 0, h))
    return pl.pallas_call(
        attend_back_kernel,
        grid=(BLOCKS,),
        in_specs=[plain] + keys + [plain, spec_probs],
        out_specs=[plain, part_spec, part_spec],
        out_shape=[jax.ShapeDtypeStruct(queries.shape, LOW), part, part],
        cost_estimate=pl.CostEstimate(
            flops=BLOCKS * 4 * rows * rows * 1024 * 2,
            bytes_accessed=16 * rows * width * 2,
            transcendentals=0,
        ),
    )(queries, own, own, other, other, mixed_grad, probs)


def matmul(left, right):
    return jnp.dot(left, right, preferred_element_type=FULL)


def normalise(values):
    average = jnp.mean(values, axis=-1, keepdims=True)
    centred = values - average
    variance = jnp.mean(centred * centred, axis=-1, keepdims=True)
    scale = lax.rsqrt(variance + 1e-05)
    return centred * scale, scale


def normalise_back(grad, gain, unit, scale):
    scaled = grad * gain
    first = jnp.mean(scaled, axis=-1, keepdims=True)
    second = jnp.mean(scaled * unit, axis=-1, keepdims=True)
    return scale * (scaled - first - unit * second)


def column_sum(values):
    if values.dtype == LOW:
        return matmul(jnp.ones((8, values.shape[0]), LOW), values)[:1]
    return jnp.sum(values, axis=0, keepdims=True)


def left_t(left, right):
    return jnp.einsum("ra,rb->ab", left, right, preferred_element_type=FULL)


def right_t(left, right):
    return jnp.einsum("ra,ba->rb", left, right, preferred_element_type=FULL)


def halves(values):
    turned_values = flip(values)
    half = values.shape[-1] // 2
    return turned_values[..., :half], turned_values[..., half:]


def unfold(parts):
    first = core_low()
    out = []
    for mine, other, pieces, size in parts:
        for j in range(pieces):
            pair = mine[:, j * size : (j + 1) * size], other[:, j * size : (j + 1) * size]
            out += [jnp.where(first, *pair), jnp.where(first, *pair[::-1])]
    return jnp.concatenate(out, axis=1)


def forward_layer(pump, hidden, layer, vectors, meta):
    inputs = hidden.astype(LOW)
    vec = vectors
    own = jnp.concatenate(
        [
            matmul(inputs, layer["key"]).astype(LOW),
            (matmul(inputs, layer["value"]) + vec["value_bias"]).astype(LOW),
        ],
        axis=1,
    )
    far = swap_core(own)
    queries = (matmul(inputs, layer["query"]) + vec["query_bias"]).astype(LOW)
    mixed, probs = attend(queries, own, far, meta)
    pre_one = hidden + (matmul(mixed, layer["out"]) + vec["out_bias"])
    unit_one, scale_one = normalise(pre_one)
    normed = unit_one * vec["first_gain"] + vec["first_shift"]
    normed_low = normed.astype(LOW)
    activated, slope = [], []
    for g in range(GROUPS):
        upward = matmul(normed_low, layer["up"][g]) + vec["up_bias"][:, g * D : (g + 1) * D]
        share = 0.5 * (1.0 + lax.erf(upward * (0.5**0.5)))
        density = jnp.exp(-0.5 * upward * upward) * 0.3989422804014327
        activated.append((upward * share).astype(LOW))
        slope.append((share + upward * density).astype(LOW))
    activated = jnp.concatenate(activated, axis=1)
    pre_two = normed + (matmul(activated, layer["down_all"]) + vec["down_bias"])
    unit_two, scale_two = normalise(pre_two)
    result = unit_two * vec["second_gain"] + vec["second_shift"]
    kept = (inputs, queries, own, far, probs, mixed, unit_one, scale_one, normed_low)
    kept += (activated, slope, unit_two, scale_two)
    return result, kept


def product(left, right):
    sent = left_t(left, right[1]).astype(LOW)
    return sent, lambda: left_t(left, right[0]).astype(LOW)


def backward_layer(pump, upstream, kept, layer, vec, last, rank, tie):
    (inputs, queries, own, far, probs, mixed, unit_one, scale_one, normed_low) = kept[:9]
    activated, slope, unit_two, scale_two = kept[9:]
    grads = {}
    streams = {}
    grads["second_gain"] = column_sum(upstream * unit_two)
    grads["second_shift"] = column_sum(upstream)
    d_two = normalise_back(upstream, vec["second_gain"], unit_two, scale_two)
    down_grad = lax.optimization_barrier(d_two.astype(LOW))
    grads["down_bias"] = column_sum(down_grad)
    first = last is not None
    if first:
        down_halves = halves(down_grad)
        streams["down"] = Scatter(*product(activated, down_halves), "narrow", rank, GROUPS)
        pump.add(streams["down"])
    up_grad = jnp.concatenate(
        [(right_t(down_grad, layer["down"][g]) * slope[g]).astype(LOW) for g in range(GROUPS)],
        axis=1,
    )
    up_grad = lax.optimization_barrier(up_grad)
    up_grad = pump.advance(8.0, up_grad)
    grads["up_bias"] = column_sum(up_grad)
    if first:
        streams["up"] = Scatter(*product(normed_low, halves(up_grad)), "wide", rank + 1)
        pump.add(streams["up"])
    else:
        parts = products(normed_low, activated, up_grad, down_grad)
        up_grad, parts = lax.optimization_barrier((up_grad, parts))
        streams["ff"] = lax.psum_scatter(
            parts, ("wide", "narrow"), scatter_dimension=0, tiled=True
        )
        pump.now += 9.0
    d_normed = d_two
    for g in range(GROUPS):
        d_normed = d_normed + right_t(up_grad[:, g * D : (g + 1) * D], layer["up"][g])
    grads["first_gain"] = column_sum(d_normed * unit_one)
    grads["first_shift"] = column_sum(d_normed)
    d_one = normalise_back(d_normed, vec["first_gain"], unit_one, scale_one)
    branch_grad = lax.optimization_barrier(d_one.astype(LOW))
    branch_grad = pump.advance(14.0, branch_grad)
    grads["out_bias"] = column_sum(branch_grad)
    branch_halves = halves(branch_grad)
    mixed_grad = right_t(branch_grad, layer["out"]).astype(LOW)
    mixed_grad = pump.advance(3.0, mixed_grad)
    query_grad, both, both_far = attend_back(queries, mixed_grad, probs, own, far)
    both_far = pump.advance(10.0, both_far)
    back = swap_core(both_far)
    grads["query_bias"] = column_sum(query_grad)
    query_halves = halves(query_grad)
    sent = [
        left_t(inputs, query_halves[1]).astype(LOW),
        left_t(mixed, branch_halves[1]).astype(LOW),
    ]
    sent[0] = pump.advance(3.0, sent[0])
    both = (both.astype(FULL) + back.astype(FULL)).astype(LOW)
    grads["value_bias"] = column_sum(both[1])
    key_halves, value_halves = halves(both[0]), halves(both[1])
    pairs = [jnp.concatenate([key_halves[i], value_halves[i]], axis=1) for i in range(2)]
    packs = last(grads) if first else None
    if first:
        sent.append(packs[1])

    def kept_part():
        parts = [left_t(inputs, query_halves[0]), left_t(mixed, branch_halves[0])]
        if first:
            parts.append(packs[0].astype(FULL))
        return jnp.concatenate(parts, axis=1).astype(LOW)

    streams["qo"] = Scatter(jnp.concatenate(sent, axis=1), kept_part, "wide", rank + 2)
    streams["kv"] = Scatter(*product(inputs, pairs), "narrow", rank + 2)
    pump.add(streams["qo"])
    pump.add(streams["kv"])
    d_input = d_one + right_t(query_grad, layer["query"])
    d_input = d_input + right_t(both[0], layer["key"]) + right_t(both[1], layer["value"])
    d_input = tie(d_input)
    d_input = pump.advance(8.0, d_input)
    return d_input, streams, grads


NAMES = (
    "query_bias",
    "value_bias",
    "out_bias",
    "down_bias",
    "first_gain",
    "first_shift",
    "second_gain",
    "second_shift",
    "up_bias",
)


GROUPS = FF // D
COUNT = 8 + GROUPS
WIDTH = 4 * D + 2 * FF


def regroup():
    share = D // (lax.axis_size("wide") * lax.axis_size("narrow"))
    devices = D // (GROUPS * share)
    order_out = np.arange(D).reshape(devices, GROUPS, share).transpose(1, 0, 2).reshape(D)
    moves = np.zeros((D, D), np.float32)
    moves[order_out, np.arange(D)] = 1.0
    return jnp.asarray(moves, LOW)


def diagonal(rows, columns):
    row = lax.broadcasted_iota(jnp.int32, (rows, columns), 0)
    return (row == lax.broadcasted_iota(jnp.int32, (rows, columns), 1)).astype(LOW)


def pack_whole(grads):
    vectors = [grads[name] for name in NAMES]

    def kernel(*refs):
        ins, out = refs[:-1], refs[-1]
        rows = [ref[...] for ref in ins[:-1]]
        rows += [ins[-1][:, g * D : (g + 1) * D] for g in range(GROUPS)]
        rows.append(jnp.zeros((16 - len(rows), D), FULL))
        stacked = jnp.concatenate(rows, axis=0).astype(LOW)
        out[...] = dot_l(stacked, diagonal(16, PAD)).astype(LOW)

    return pl.pallas_call(
        kernel,
        out_shape=jax.ShapeDtypeStruct((D, PAD), LOW),
    )(*vectors)


def unpack_whole(core, mine, other):
    def kernel(core_ref, mine_ref, other_ref, *outs):
        def write(order_of):
            for index, ref in enumerate(order_of):
                rows = dot_t(diagonal(16, PAD), ref[...])
                outs[2 * index][...] = rows
                for g in range(GROUPS):
                    outs[2 * index + 1][:, g * D : (g + 1) * D] = rows[8 + g : 9 + g]

        @pl.when(core_ref[0] == 0)
        def _():
            write((mine_ref, other_ref))

        @pl.when(core_ref[0] != 0)
        def _():
            write((other_ref, mine_ref))

    spec = pl.BlockSpec(memory_space=pltpu.VMEM)
    outs = pl.pallas_call(
        kernel,
        in_specs=[pl.BlockSpec(memory_space=pltpu.SMEM), spec, spec],
        out_shape=[jax.ShapeDtypeStruct((16, D), FULL), jax.ShapeDtypeStruct((1, FF), FULL)] * 2,
    )(core, mine, other)
    out = []
    for index in range(LAYERS):
        rows = outs[2 * index]
        vectors = {name: rows[i : i + 1] for i, name in enumerate(NAMES[:-1])}
        vectors["up_bias"] = outs[2 * index + 1]
        out.append(vectors)
    return out


def group_columns(values, moves, back=False):
    cut = D // GROUPS
    if not back:
        parts = [
            jnp.dot(values[:, q * D : (q + 1) * D], moves, preferred_element_type=FULL)
            for q in range(GROUPS)
        ]
        return [
            jnp.concatenate([part[:, g * cut : (g + 1) * cut] for part in parts], axis=1)
            for g in range(GROUPS)
        ]
    out = []
    for q in range(GROUPS):
        part = [values[:, g * D + q * cut : g * D + (q + 1) * cut] for g in range(GROUPS)]
        out.append(dot_t(jnp.concatenate(part, axis=1), moves))
    return out


def pack_shards(core, weights, vectors, moves):
    query, key, value, out, up, down = weights
    share = query.shape[1]
    names = list(NAMES)

    def kernel(core_ref, q_ref, k_ref, v_ref, o_ref, u_ref, d_ref, moves_ref, *refs):
        ins, (mine_ref, sent_ref, whole_ref) = refs[:-3], refs[-3:]
        for j, ref in enumerate((k_ref, v_ref, q_ref, o_ref)):
            whole_ref[j] = ref[1]
        packs = []
        for index in range(LAYERS):
            base = 4 + index * 2 * GROUPS
            for g, part in enumerate(group_columns(u_ref[index], moves_ref[...])):
                whole_ref[base + g] = part.astype(LOW)
            for g in range(GROUPS):
                whole_ref[base + GROUPS + g] = d_ref[index, g * share : (g + 1) * share]
            rows = [ref[index : index + 1].astype(FULL) for ref in ins[:-1]]
            for g in range(GROUPS):
                rows.append(ins[-1][index : index + 1, g * share : (g + 1) * share].astype(FULL))
            rows.append(jnp.zeros((PAD - len(rows), share), FULL))
            packs.append(jnp.concatenate(rows, axis=0).T.astype(LOW))

        def write(target, side):
            for j, ref in enumerate((k_ref, v_ref, q_ref, o_ref)):
                target[:, j * HALF : (j + 1) * HALF] = ref[0, :, side * HALF : (side + 1) * HALF]
            target[:, 4 * HALF :] = packs[side]

        @pl.when(core_ref[0] == 0)
        def _():
            write(mine_ref, 0)
            write(sent_ref, 1)

        @pl.when(core_ref[0] != 0)
        def _():
            write(mine_ref, 1)
            write(sent_ref, 0)

    spec = pl.BlockSpec(memory_space=pltpu.VMEM)
    half = jax.ShapeDtypeStruct((share, 4 * HALF + PAD), LOW)
    return pl.pallas_call(
        kernel,
        in_specs=[pl.BlockSpec(memory_space=pltpu.SMEM)] + [spec] * (7 + len(names)),
        out_shape=[half, half, jax.ShapeDtypeStruct((4 + 4 * GROUPS, share, D), LOW)],
    )(core, *weights, moves, *[vectors[name] for name in names])


def join_rows(core, mine, other, cuts):
    def kernel(core_ref, mine_ref, other_ref, *outs):
        for (start, size), out in zip(cuts, outs):
            out[core_ref[0]] = mine_ref[:, start : start + size]
            out[1 - core_ref[0]] = other_ref[:, start : start + size]

    spec = pl.BlockSpec(memory_space=pltpu.VMEM)
    return pl.pallas_call(
        kernel,
        in_specs=[pl.BlockSpec(memory_space=pltpu.SMEM), spec, spec],
        out_shape=[jax.ShapeDtypeStruct((2, mine.shape[0], size), LOW) for _, size in cuts],
    )(core, mine, other)


def unpack_shards(core, first, second, moves):
    share = second.shape[0]

    def kernel(core_ref, second_ref, moves_ref, *refs):
        group, outs = refs[:4], refs[4:]
        grouped = second_ref[:, :FF]
        for q, part in enumerate(group_columns(grouped, moves_ref[...], back=True)):
            outs[4][1, :, q * D : (q + 1) * D] = part
        for g in range(GROUPS):
            start = (GROUPS + g) * D
            outs[5][1, g * share : (g + 1) * share] = second_ref[:, start : start + D].astype(FULL)

        def write(flipped):
            for side in range(2):
                rows = group[side ^ flipped]
                downs = group[2 + (side ^ flipped)]
                cut = slice(side * HALF, (side + 1) * HALF)
                tail = 4 * HALF + FF // 2
                for j, place in enumerate((0, 3, 1, 2)):
                    outs[place][0, :, cut] = rows[:, j * HALF : (j + 1) * HALF].astype(FULL)
                    start = tail + PAD + j * HALF
                    outs[place][1, :, cut] = rows[:, start : start + HALF].astype(FULL)
                outs[6][side] = rows[:, tail : tail + PAD].astype(FULL).T
                for g in range(GROUPS):
                    place = slice(g * share, (g + 1) * share)
                    outs[5][0, place, cut] = downs[place].astype(FULL)
            ups = [group[side ^ flipped][:, 4 * HALF : 4 * HALF + FF // 2] for side in range(2)]
            ups = group_columns(jnp.concatenate(ups, axis=1), moves_ref[...], back=True)
            for q, part in enumerate(ups):
                outs[4][0, :, q * D : (q + 1) * D] = part

        @pl.when(core_ref[0] == 0)
        def _():
            write(0)

        @pl.when(core_ref[0] != 0)
        def _():
            write(1)

    spec = pl.BlockSpec(memory_space=pltpu.VMEM)
    shapes = [(share, D)] * 4 + [(share, FF), (GROUPS * share, D), (PAD, share)]
    *weights, rows = pl.pallas_call(
        kernel,
        in_specs=[pl.BlockSpec(memory_space=pltpu.SMEM)] + [spec] * (2 + len(first)),
        out_shape=[jax.ShapeDtypeStruct((LAYERS,) + shape, FULL) for shape in shapes],
    )(core, second, moves, *first)
    vectors = {name: rows[:, i] for i, name in enumerate(NAMES[:-1])}
    vectors["up_bias"] = rows[:, 8 : 8 + GROUPS].reshape(LAYERS, -1)
    return weights, vectors


def products(normed, activated, up, down):
    rows = normed.shape[0]
    steps = 2 * GROUPS

    def kernel(normed_ref, act_ref, up_ref, down_ref, out):
        step = pl.program_id(0)

        @pl.when(step < GROUPS)
        def _():
            out[...] = dot_l(normed_ref[...], up_ref[...]).astype(LOW)

        @pl.when(step >= GROUPS)
        def _():
            out[...] = dot_l(act_ref[...], down_ref[...]).astype(LOW)

    def at(low):
        return pl.BlockSpec((rows, D), lambda i: (0, jnp.clip(i - low, 0, GROUPS - 1)))

    whole = pl.BlockSpec((rows, D), lambda i: (0, 0))
    return pl.pallas_call(
        kernel,
        grid=(steps,),
        in_specs=[whole, at(GROUPS), at(0), whole],
        out_specs=pl.BlockSpec((D, D), lambda i: (0, i)),
        out_shape=jax.ShapeDtypeStruct((D, steps * D), LOW),
        cost_estimate=pl.CostEstimate(
            flops=2 * rows * D * D * steps, bytes_accessed=D * D * steps * 2, transcendentals=0
        ),
    )(normed, activated, up, down)


def body(
    tokens,
    query_weight,
    key_weight,
    value_weight,
    out_weight,
    up_weight,
    down_weight,
    query_bias,
    value_bias,
    out_bias,
    up_bias,
    down_bias,
    first_gain,
    first_shift,
    second_gain,
    second_shift,
    lengths,
    cotangent,
):
    pairs, rows_pair, width = tokens.shape
    given = dict(
        query_bias=query_bias,
        value_bias=value_bias,
        out_bias=out_bias,
        up_bias=up_bias,
        down_bias=down_bias,
        first_gain=first_gain,
        first_shift=first_shift,
        second_gain=second_gain,
        second_shift=second_shift,
    )
    core = own_bit("narrow", 0).astype(jnp.int32).reshape(1)
    side_x = own_bit("narrow", 1)
    moves = regroup()
    mine, sent, shard = pack_shards(
        core,
        (query_weight, key_weight, value_weight, out_weight, up_weight, down_weight),
        given,
        moves,
    )
    other = swap_core(sent)
    whole = lax.all_gather(shard, ("wide", "narrow"), axis=1, tiled=True)
    kv_0, qo_0 = join_rows(core, mine, other, [(0, D), (D, D + PAD)])
    pump = Pump()
    pump.now = 13.0
    gathers = [Gather(kv_0, "wide", 0), Gather(qo_0, "narrow", 0)]
    for stream in gathers:
        pump.add(stream)

    def collect(values, rank):
        keep = lax.dynamic_index_in_dim(values, side_x, 0, keepdims=False)
        sent = lax.dynamic_index_in_dim(values, 1 - side_x, 0, keepdims=False)
        stream = Exchange(sent, 1, rank)
        pump.add(stream)

        def joined():
            pump.need([stream])
            return jnp.concatenate([keep, stream.other], axis=0)

        return joined

    def hand_back(values, rank):
        mine = values[:rows_pair]
        stream = Exchange(values[rows_pair:], 1, rank)
        pump.add(stream)
        first = side_x == 0
        return stream, lambda: jnp.stack(
            [jnp.where(first, mine, stream.other), jnp.where(first, stream.other, mine)], axis=0
        )

    narrow = lax.axis_index("narrow")
    scalars = [lax.dynamic_index_in_dim(lengths, side_x, 0, keepdims=False)]
    scalars += [(narrow ^ j) * rows_pair for j in (0, 2, 1, 3)]
    meta = jnp.stack([value.astype(jnp.int32) for value in scalars])

    hidden = collect(tokens, -1)
    upstream = collect(cotangent, 9)
    pump.need(gathers)
    parts = [(stream.mine, stream.other, 2, HALF) for stream in gathers]
    kv, qo = unfold(parts[:1]), unfold(parts[1:])
    first_pieces = dict(key=kv[:, :D], value=kv[:, D:], query=qo[:, :D], out=qo[:, D:])
    second_pieces = dict(key=whole[0], value=whole[1], query=whole[2], out=whole[3])
    layers = []
    for index, pieces in enumerate((first_pieces, second_pieces)):
        base = 4 + index * 2 * GROUPS
        pieces["up"] = [whole[base + g] for g in range(GROUPS)]
        down = whole[base + GROUPS : base + 2 * GROUPS]
        pieces["down"] = [down[g] for g in range(GROUPS)]
        pieces["down_all"] = down.reshape(FF, D)
        layers.append(pieces)
    vectors = unpack_whole(core, gathers[1].mine[:, D:], gathers[1].other[:, D:])
    kept = []
    hidden = hidden().astype(FULL)
    for index in range(LAYERS):
        hidden, saved = forward_layer(
            pump, hidden, layers[index], vectors[index], meta
        )
        kept.append(saved)
    output = hand_back(hidden.astype(LOW), 9)
    grads = [None] * LAYERS
    scatters = [None] * LAYERS

    def pack_all(first_grads):
        low, high = pack_whole(first_grads), pack_whole(grads[1])
        first = core_low()
        return jnp.where(first, low, high), jnp.where(first, high, low)

    upstream = upstream().astype(FULL)

    def hold(value):
        value, scatters[1]["ff"] = lax.optimization_barrier((value, scatters[1]["ff"]))
        return value

    for index in reversed(range(LAYERS)):
        upstream, scatters[index], grads[index] = backward_layer(
            pump,
            upstream,
            kept[index],
            layers[index],
            vectors[index],
            pack_all if index == 0 else None,
            0 if index == 1 else 4,
            hold if index == 0 else lambda value: value,
        )
    tokens_grad = hand_back(upstream.astype(LOW), 9)
    second_ff = scatters[1].pop("ff")
    for streams in scatters[::-1]:
        pump.need(streams.values())
    streams = scatters[0]
    rows = [streams[name].result[0] for name in ("qo", "kv", "up")]
    rows = [rows[0][:, :D], rows[1], rows[2], rows[0][:, D:]]
    rows += [scatters[1][name].result[0] for name in ("qo", "kv")]
    rows = jnp.concatenate(rows, axis=1)
    ends = []
    downs = streams["down"].result
    share = downs.shape[1] // 2
    downs = downs.reshape(GROUPS, 2, share, HALF).transpose(1, 0, 2, 3)
    for values in (rows, downs):
        split = values.reshape(2, -1, values.shape[-1])
        mine = lax.dynamic_index_in_dim(split, core[0], 0, keepdims=False)
        sent = lax.dynamic_index_in_dim(split, 1 - core[0], 0, keepdims=False)
        ends += [mine, swap_core(sent)]
    weight_grads, small = unpack_shards(core, ends, second_ff, moves)
    pump.need([output[0], tokens_grad[0]])
    names = (
        "query_bias",
        "value_bias",
        "out_bias",
        "up_bias",
        "down_bias",
        "first_gain",
        "first_shift",
        "second_gain",
        "second_shift",
    )
    return (output[1](), tokens_grad[1](), *weight_grads, *[small[name] for name in names])


def solution(mesh):
    rows = P("wide", "narrow", None)
    weight = P(None, ("wide", "narrow"), None)
    vector = P(None, ("wide", "narrow"))
    return jax.shard_map(
        body,
        mesh=mesh,
        in_specs=(rows,) + (weight,) * 6 + (vector,) * 9 + (P("wide"), rows),
        out_specs=(rows, rows) + (weight,) * 6 + (vector,) * 9,
        check_vma=False,
    )
```

```python
import functools
import heapq

import jax
import jax.numpy as jnp
from jax import lax
from jax.experimental import pallas as pl
from jax.experimental.pallas import tpu as pltpu
import numpy as np
from jax.sharding import PartitionSpec as P

D = 768
HEADS = 12
HD = 64
FF = 3072
LAYERS = 2
PAD = 128
HALF = D // 2
LOW = jnp.bfloat16
FULL = jnp.float32


def bits_of(name):
    return lax.axis_size(name).bit_length() - 1


def swap(value, name, bit):
    pairs = [(i, i ^ (1 << bit)) for i in range(lax.axis_size(name))]
    return lax.ppermute(value, name, pairs)


def swap_core(value):
    return swap(value, "narrow", 0)


def own_bit(name, bit):
    return (lax.axis_index(name) >> bit) & 1


def core_low():
    return own_bit("narrow", 0) == 0


def axis_of(name, bit):
    if name == "wide":
        return bits_of("wide") - 1 - bit
    return bits_of("wide")


def order(first):
    far = [("wide", bit) for bit in range(bits_of("wide") - 1, 0, -1)]
    middle = [("wide", 0), ("narrow", 1)]
    if first == "narrow":
        middle.reverse()
    return far + middle


def flip(values):
    half = values.shape[-1] // 2
    turned = jnp.concatenate([values[..., half:], values[..., :half]], axis=-1)
    return jnp.where(core_low(), values, turned)


def link_of(name, bit):
    if name == "narrow":
        return "x"
    return "y" if bit == 0 else "z"


RATE = 40e3
BACK_RATE = 12e3
CORE_RATE = 500e3
COPY_RATE = 1.0e6
START = 1.5
STEP = 0.8


class Gather:
    def __init__(self, shard, first, rank):
        self.stages = order(first) + [("core", 0)]
        lead = bits_of("wide") + 1
        self.held = shard.reshape((1,) * lead + shard.shape)
        self.rank = rank
        self.done = False

    def link(self, k):
        name, bit = self.stages[k]
        return "core" if name == "core" else link_of(name, bit)

    def time(self, k):
        name, bit = self.stages[k]
        size = self.held.size * 2
        if name == "core":
            return size / CORE_RATE
        return size / RATE * (2 if name == "wide" and bit > 1 else 1)

    def operand(self, k):
        if self.stages[k][0] == "core":
            self.held = self.held.reshape(-1, self.held.shape[-1])
        return self.held

    def send(self, k, value):
        self.held = value
        name, bit = self.stages[k]
        return swap_core(value) if name == "core" else swap(value, name, bit)

    def finish(self, k, other):
        name, bit = self.stages[k]
        if name == "core":
            self.mine, self.other = self.held, other
            self.done = True
            return 0.0
        axis = axis_of(name, bit)
        shape = self.held.shape[:axis] + (2,) + self.held.shape[axis + 1 :]
        place = lax.broadcasted_iota(jnp.int32, shape, axis)
        self.held = jnp.where(place == own_bit(name, bit), self.held, other)
        return STEP + self.held.size * 4 / COPY_RATE


class Scatter:
    def __init__(self, sent, kept, first, rank, groups=1):
        self.groups = groups
        self.stages = [("core", 0)] + order(first)[::-1]
        self.sent, self.kept = sent, kept
        self.rank = rank
        self.done = False

    def link(self, k):
        name, bit = self.stages[k]
        return "core" if name == "core" else link_of(name, bit)

    def time(self, k):
        name, bit = self.stages[k]
        size = self.sent.size * 2
        if name == "core":
            return size / CORE_RATE
        return size / BACK_RATE * (2 if name == "wide" and bit > 1 else 1)

    def operand(self, k):
        return self.sent

    def send(self, k, value):
        name, bit = self.stages[k]
        return swap_core(value) if name == "core" else swap(value, name, bit)

    def finish(self, k, other):
        cost = 2 * STEP + other.size * 6 / COPY_RATE
        if k == 0:
            self.kept = self.kept()
            cost += STEP + other.size * 2 / COPY_RATE
            chips = lax.axis_size("wide") * lax.axis_size("narrow") // 2
            shape = (self.groups,) + (2,) * (bits_of("wide") + 1)
            shape += (other.shape[0] // (chips * self.groups), other.shape[1])
            self.kept, other = self.kept.reshape(shape), other.reshape(shape)
        if k + 1 == len(self.stages):
            total = self.kept.astype(FULL) + other.astype(FULL)
            self.result = total.astype(LOW).reshape(-1, *total.shape[-2:])
            self.done = True
            return cost
        name, bit = self.stages[k + 1]
        axis, mine = 1 + axis_of(name, bit), own_bit(name, bit)

        def part(which):
            cut = [lax.dynamic_index_in_dim(value, which, axis) for value in (self.kept, other)]
            return (cut[0].astype(FULL) + cut[1].astype(FULL)).astype(LOW)

        self.sent, self.kept = part(1 - mine), part(mine)
        return cost


class Exchange:
    def __init__(self, value, bit, rank):
        self.value, self.bit, self.rank = value, bit, rank
        self.done = False

    def link(self, k):
        return "core" if self.bit == 0 else "x"

    def time(self, k):
        return self.value.size * 2 / (CORE_RATE if self.bit == 0 else RATE)

    def operand(self, k):
        return self.value

    def send(self, k, value):
        self.value = value
        return swap(value, "narrow", self.bit)

    def finish(self, k, other):
        self.other = other
        self.done = True
        return 0.0


class Pump:
    def __init__(self, depth=3):
        self.now = 0.0
        self.depth = depth
        self.flying = []
        self.links = {}
        self.count = 0
        self.last = None
        self.sent = None
        self.value = None

    def add(self, stream):
        self.request(stream, 0)

    def request(self, stream, k):
        link = self.links.setdefault(stream.link(k), [0, 0.0, []])
        if link[0] < self.depth:
            self.issue(stream, k, link)
        else:
            self.count += 1
            heapq.heappush(link[2], (stream.rank, self.count, stream, k))

    def issue(self, stream, k, link):
        operand = stream.operand(k)
        for other in (self.last, self.sent):
            if other is not None:
                operand, _ = lax.optimization_barrier((operand, other))
        self.sent = operand
        if self.value is not None:
            operand, self.value = lax.optimization_barrier((operand, self.value))
        link[0] += 1
        self.now += 0.3 if stream.link(k) == "core" else START
        end = max(self.now, link[1]) + stream.time(k) + 0.7
        link[1] = end - 0.7
        other = stream.send(k, operand)
        if stream.link(k) == "core":
            self.sent = other
        self.count += 1
        heapq.heappush(self.flying, (end, self.count, stream, k, other))

    def step(self):
        end, _, stream, k, other = heapq.heappop(self.flying)
        self.now = max(self.now, end)
        link = self.links[stream.link(k)]
        link[0] -= 1
        self.last = other
        self.now += stream.finish(k, other)
        if not stream.done:
            self.request(stream, k + 1)
        if link[2] and link[0] < self.depth:
            _, _, waiting, j = heapq.heappop(link[2])
            self.issue(waiting, j, link)

    def advance(self, time, value):
        self.value = value
        self.now += time
        while self.flying and self.flying[0][0] <= self.now:
            self.step()
        value, self.value = self.value, None
        return value

    def idle(self, time):
        while self.flying and self.flying[0][0] <= time:
            self.step()
        self.now = max(self.now, time)

    def need(self, streams, value=None):
        self.value = value
        while not all(stream.done for stream in streams):
            self.step()
        value, self.value = self.value, None
        return value


BLOCKS = D // 128


def stack_heads(pair):
    lane = lax.broadcasted_iota(jnp.int32, pair.shape, 1)
    zero = jnp.zeros_like(pair)
    return jnp.concatenate(
        [jnp.where(lane < HD, pair, zero), jnp.where(lane < HD, zero, pair)], axis=0
    )


def pick_heads(stacked):
    rows = stacked.shape[0] // 2
    lane = lax.broadcasted_iota(jnp.int32, (rows, stacked.shape[1]), 1)
    return jnp.where(lane < HD, stacked[:rows], stacked[rows:])


def dot_t(left, right):
    return lax.dot_general(left, right, (((1,), (1,)), ((), ())), preferred_element_type=FULL)


def dot_l(left, right):
    return lax.dot_general(left, right, (((0,), (0,)), ((), ())), preferred_element_type=FULL)


def attend_kernel(meta, query, key_own, value_own, key_other, value_other, mixed, probs):
    length = meta[0]
    stacked = stack_heads(query[...])
    keys = jnp.concatenate([key_own[...], key_other[...]], axis=0)
    scores = dot_t(stacked, keys) * HD**-0.5
    rows = keys.shape[0] // 4
    column = lax.broadcasted_iota(jnp.int32, (1, keys.shape[0]), 1)
    place = column + meta[1]
    for j in range(1, 4):
        place = jnp.where(column >= j * rows, column - j * rows + meta[1 + j], place)
    scores = jnp.where(place < length, scores, -1e30)
    raised = jnp.exp(scores - jnp.max(scores, axis=1, keepdims=True))
    low = (raised / jnp.sum(raised, axis=1, keepdims=True)).astype(LOW)
    probs[0] = low
    values = jnp.concatenate([value_own[...], value_other[...]], axis=0)
    mixed[...] = pick_heads(jnp.dot(low, values, preferred_element_type=FULL)).astype(LOW)


def specs(rows):
    def at(index):
        return pl.BlockSpec((rows, 128), index)

    plain = at(lambda h, *_: (0, h))
    far = at(lambda h, *_: (0, BLOCKS + h))
    probs = pl.BlockSpec((1, 2 * rows, 2 * rows), lambda h, *_: (h, 0, 0))
    return plain, [plain, far, plain, far], probs


def attend(queries, own, other, meta):
    rows, width = queries.shape
    plain, keys, probs = specs(rows)
    return pl.pallas_call(
        attend_kernel,
        grid_spec=pltpu.PrefetchScalarGridSpec(
            num_scalar_prefetch=1,
            grid=(BLOCKS,),
            in_specs=[plain] + keys,
            out_specs=[plain, probs],
        ),
        out_shape=[
            jax.ShapeDtypeStruct(queries.shape, LOW),
            jax.ShapeDtypeStruct((BLOCKS, 2 * rows, 2 * rows), LOW),
        ],
        cost_estimate=pl.CostEstimate(
            flops=BLOCKS * 4 * rows * rows * 512 * 2,
            bytes_accessed=8 * rows * width * 2,
            transcendentals=BLOCKS * 4 * rows * rows,
        ),
    )(meta, queries, own, own, other, other)


def attend_back_kernel(
    query,
    key_own,
    value_own,
    key_other,
    value_other,
    mixed_grad,
    probs,
    query_grad,
    both_grad,
    both_grad_other,
):
    rows = query.shape[0]
    queries = stack_heads(query[...])
    grads = stack_heads(mixed_grad[...])
    low = probs[0]
    keys = jnp.concatenate([key_own[...], key_other[...]], axis=0)
    values = jnp.concatenate([value_own[...], value_other[...]], axis=0)
    prob_grad = dot_t(grads, values)
    wide = low.astype(FULL)
    weighted = jnp.sum(wide * prob_grad, axis=1, keepdims=True)
    score_grad = (wide * (prob_grad - weighted)).astype(LOW)
    query_grad[...] = (
        pick_heads(jnp.dot(score_grad, keys, preferred_element_type=FULL)) * HD**-0.5
    ).astype(LOW)
    key_all = (dot_l(score_grad, queries) * HD**-0.5).astype(LOW)
    value_all = dot_l(low, grads).astype(LOW)
    both_grad[0] = key_all[:rows]
    both_grad[1] = value_all[:rows]
    both_grad_other[0] = key_all[rows:]
    both_grad_other[1] = value_all[rows:]


def attend_back(queries, mixed_grad, probs, own, other):
    rows, width = queries.shape
    plain, keys, spec_probs = specs(rows)
    part = jax.ShapeDtypeStruct((2, rows, width), LOW)
    part_spec = pl.BlockSpec((2, rows, 128), lambda h: (0, 0, h))
    return pl.pallas_call(
        attend_back_kernel,
        grid=(BLOCKS,),
        in_specs=[plain] + keys + [plain, spec_probs],
        out_specs=[plain, part_spec, part_spec],
        out_shape=[jax.ShapeDtypeStruct(queries.shape, LOW), part, part],
        cost_estimate=pl.CostEstimate(
            flops=BLOCKS * 4 * rows * rows * 1024 * 2,
            bytes_accessed=16 * rows * width * 2,
            transcendentals=0,
        ),
    )(queries, own, own, other, other, mixed_grad, probs)


def matmul(left, right):
    return jnp.dot(left, right, preferred_element_type=FULL)


def normalise(values):
    average = jnp.mean(values, axis=-1, keepdims=True)
    centred = values - average
    variance = jnp.mean(centred * centred, axis=-1, keepdims=True)
    scale = lax.rsqrt(variance + 1e-05)
    return centred * scale, scale


def normalise_back(grad, gain, unit, scale):
    scaled = grad * gain
    first = jnp.mean(scaled, axis=-1, keepdims=True)
    second = jnp.mean(scaled * unit, axis=-1, keepdims=True)
    return scale * (scaled - first - unit * second)


def column_sum(values):
    if values.dtype == LOW:
        return matmul(jnp.ones((8, values.shape[0]), LOW), values)[:1]
    return jnp.sum(values, axis=0, keepdims=True)


def left_t(left, right):
    return jnp.einsum("ra,rb->ab", left, right, preferred_element_type=FULL)


def right_t(left, right):
    return jnp.einsum("ra,ba->rb", left, right, preferred_element_type=FULL)


def halves(values):
    turned_values = flip(values)
    half = values.shape[-1] // 2
    return turned_values[..., :half], turned_values[..., half:]


def unfold(parts):
    first = core_low()
    out = []
    for mine, other, pieces, size in parts:
        for j in range(pieces):
            pair = mine[:, j * size : (j + 1) * size], other[:, j * size : (j + 1) * size]
            out += [jnp.where(first, *pair), jnp.where(first, *pair[::-1])]
    return jnp.concatenate(out, axis=1)


def forward_layer(pump, hidden, layer, vectors, meta):
    inputs = hidden.astype(LOW)
    vec = vectors
    own = jnp.concatenate(
        [
            matmul(inputs, layer["key"]).astype(LOW),
            (matmul(inputs, layer["value"]) + vec["value_bias"]).astype(LOW),
        ],
        axis=1,
    )
    far = swap_core(own)
    queries = (matmul(inputs, layer["query"]) + vec["query_bias"]).astype(LOW)
    mixed, probs = attend(queries, own, far, meta)
    pre_one = hidden + (matmul(mixed, layer["out"]) + vec["out_bias"])
    unit_one, scale_one = normalise(pre_one)
    normed = unit_one * vec["first_gain"] + vec["first_shift"]
    normed_low = normed.astype(LOW)
    activated, slope = [], []
    for g in range(GROUPS):
        upward = matmul(normed_low, layer["up"][g]) + vec["up_bias"][:, g * D : (g + 1) * D]
        share = 0.5 * (1.0 + lax.erf(upward * (0.5**0.5)))
        density = jnp.exp(-0.5 * upward * upward) * 0.3989422804014327
        activated.append((upward * share).astype(LOW))
        slope.append((share + upward * density).astype(LOW))
    activated = jnp.concatenate(activated, axis=1)
    pre_two = normed + (matmul(activated, layer["down_all"]) + vec["down_bias"])
    unit_two, scale_two = normalise(pre_two)
    result = unit_two * vec["second_gain"] + vec["second_shift"]
    kept = (inputs, queries, own, far, probs, mixed, unit_one, scale_one, normed_low)
    kept += (activated, slope, unit_two, scale_two)
    return result, kept


def product(left, right):
    sent = left_t(left, right[1]).astype(LOW)
    return sent, lambda: left_t(left, right[0]).astype(LOW)


def backward_layer(pump, upstream, kept, layer, vec, last, rank, tie):
    (inputs, queries, own, far, probs, mixed, unit_one, scale_one, normed_low) = kept[:9]
    activated, slope, unit_two, scale_two = kept[9:]
    grads = {}
    streams = {}
    grads["second_gain"] = column_sum(upstream * unit_two)
    grads["second_shift"] = column_sum(upstream)
    d_two = normalise_back(upstream, vec["second_gain"], unit_two, scale_two)
    down_grad = lax.optimization_barrier(d_two.astype(LOW))
    grads["down_bias"] = column_sum(down_grad)
    first = last is not None
    if first:
        down_halves = halves(down_grad)
        streams["down"] = Scatter(*product(activated, down_halves), "narrow", rank, GROUPS)
        pump.add(streams["down"])
    up_grad = jnp.concatenate(
        [(right_t(down_grad, layer["down"][g]) * slope[g]).astype(LOW) for g in range(GROUPS)],
        axis=1,
    )
    up_grad = lax.optimization_barrier(up_grad)
    up_grad = pump.advance(8.0, up_grad)
    grads["up_bias"] = column_sum(up_grad)
    if first:
        streams["up"] = Scatter(*product(normed_low, halves(up_grad)), "wide", rank + 1)
        pump.add(streams["up"])
    else:
        parts = products(normed_low, activated, up_grad, down_grad)
        up_grad, parts = lax.optimization_barrier((up_grad, parts))
        streams["ff"] = lax.psum_scatter(
            parts, ("wide", "narrow"), scatter_dimension=0, tiled=True
        )
        pump.now += 9.0
    d_normed = d_two
    for g in range(GROUPS):
        d_normed = d_normed + right_t(up_grad[:, g * D : (g + 1) * D], layer["up"][g])
    grads["first_gain"] = column_sum(d_normed * unit_one)
    grads["first_shift"] = column_sum(d_normed)
    d_one = normalise_back(d_normed, vec["first_gain"], unit_one, scale_one)
    branch_grad = lax.optimization_barrier(d_one.astype(LOW))
    branch_grad = pump.advance(14.0, branch_grad)
    grads["out_bias"] = column_sum(branch_grad)
    branch_halves = halves(branch_grad)
    mixed_grad = right_t(branch_grad, layer["out"]).astype(LOW)
    mixed_grad = pump.advance(3.0, mixed_grad)
    query_grad, both, both_far = attend_back(queries, mixed_grad, probs, own, far)
    both_far = pump.advance(10.0, both_far)
    back = swap_core(both_far)
    grads["query_bias"] = column_sum(query_grad)
    query_halves = halves(query_grad)
    sent = [
        left_t(inputs, query_halves[1]).astype(LOW),
        left_t(mixed, branch_halves[1]).astype(LOW),
    ]
    sent[0] = pump.advance(3.0, sent[0])
    both = (both.astype(FULL) + back.astype(FULL)).astype(LOW)
    grads["value_bias"] = column_sum(both[1])
    key_halves, value_halves = halves(both[0]), halves(both[1])
    pairs = [jnp.concatenate([key_halves[i], value_halves[i]], axis=1) for i in range(2)]
    packs = last(grads) if first else None
    if first:
        sent.append(packs[1])

    def kept_part():
        parts = [left_t(inputs, query_halves[0]), left_t(mixed, branch_halves[0])]
        if first:
            parts.append(packs[0].astype(FULL))
        return jnp.concatenate(parts, axis=1).astype(LOW)

    streams["qo"] = Scatter(jnp.concatenate(sent, axis=1), kept_part, "wide", rank + 2)
    streams["kv"] = Scatter(*product(inputs, pairs), "narrow", rank + 2)
    pump.add(streams["qo"])
    pump.add(streams["kv"])
    d_input = d_one + right_t(query_grad, layer["query"])
    d_input = d_input + right_t(both[0], layer["key"]) + right_t(both[1], layer["value"])
    d_input = tie(d_input)
    d_input = pump.advance(8.0, d_input)
    return d_input, streams, grads


NAMES = (
    "query_bias",
    "value_bias",
    "out_bias",
    "down_bias",
    "first_gain",
    "first_shift",
    "second_gain",
    "second_shift",
    "up_bias",
)


GROUPS = FF // D
COUNT = 8 + GROUPS
WIDTH = 4 * D + 2 * FF


def regroup():
    share = D // (lax.axis_size("wide") * lax.axis_size("narrow"))
    devices = D // (GROUPS * share)
    order_out = np.arange(D).reshape(devices, GROUPS, share).transpose(1, 0, 2).reshape(D)
    moves = np.zeros((D, D), np.float32)
    moves[order_out, np.arange(D)] = 1.0
    return jnp.asarray(moves, LOW)


def diagonal(rows, columns):
    row = lax.broadcasted_iota(jnp.int32, (rows, columns), 0)
    return (row == lax.broadcasted_iota(jnp.int32, (rows, columns), 1)).astype(LOW)


def pack_whole(grads):
    vectors = [grads[name] for name in NAMES]

    def kernel(*refs):
        ins, out = refs[:-1], refs[-1]
        rows = [ref[...] for ref in ins[:-1]]
        rows += [ins[-1][:, g * D : (g + 1) * D] for g in range(GROUPS)]
        rows.append(jnp.zeros((16 - len(rows), D), FULL))
        stacked = jnp.concatenate(rows, axis=0).astype(LOW)
        out[...] = dot_l(stacked, diagonal(16, PAD)).astype(LOW)

    return pl.pallas_call(
        kernel,
        out_shape=jax.ShapeDtypeStruct((D, PAD), LOW),
    )(*vectors)


def unpack_whole(core, mine, other):
    def kernel(core_ref, mine_ref, other_ref, *outs):
        def write(order_of):
            for index, ref in enumerate(order_of):
                rows = dot_t(diagonal(16, PAD), ref[...])
                outs[2 * index][...] = rows
                for g in range(GROUPS):
                    outs[2 * index + 1][:, g * D : (g + 1) * D] = rows[8 + g : 9 + g]

        @pl.when(core_ref[0] == 0)
        def _():
            write((mine_ref, other_ref))

        @pl.when(core_ref[0] != 0)
        def _():
            write((other_ref, mine_ref))

    spec = pl.BlockSpec(memory_space=pltpu.VMEM)
    outs = pl.pallas_call(
        kernel,
        in_specs=[pl.BlockSpec(memory_space=pltpu.SMEM), spec, spec],
        out_shape=[jax.ShapeDtypeStruct((16, D), FULL), jax.ShapeDtypeStruct((1, FF), FULL)] * 2,
    )(core, mine, other)
    out = []
    for index in range(LAYERS):
        rows = outs[2 * index]
        vectors = {name: rows[i : i + 1] for i, name in enumerate(NAMES[:-1])}
        vectors["up_bias"] = outs[2 * index + 1]
        out.append(vectors)
    return out


def group_columns(values, moves, back=False):
    cut = D // GROUPS
    if not back:
        parts = [
            jnp.dot(values[:, q * D : (q + 1) * D], moves, preferred_element_type=FULL)
            for q in range(GROUPS)
        ]
        return [
            jnp.concatenate([part[:, g * cut : (g + 1) * cut] for part in parts], axis=1)
            for g in range(GROUPS)
        ]
    out = []
    for q in range(GROUPS):
        part = [values[:, g * D + q * cut : g * D + (q + 1) * cut] for g in range(GROUPS)]
        out.append(dot_t(jnp.concatenate(part, axis=1), moves))
    return out


def pack_shards(core, weights, vectors, moves):
    query, key, value, out, up, down = weights
    share = query.shape[1]
    names = list(NAMES)

    def kernel(core_ref, q_ref, k_ref, v_ref, o_ref, u_ref, d_ref, moves_ref, *refs):
        ins, (mine_ref, sent_ref, whole_ref) = refs[:-3], refs[-3:]
        for j, ref in enumerate((k_ref, v_ref, q_ref, o_ref)):
            whole_ref[j] = ref[1]
        packs = []
        for index in range(LAYERS):
            base = 4 + index * 2 * GROUPS
            for g, part in enumerate(group_columns(u_ref[index], moves_ref[...])):
                whole_ref[base + g] = part.astype(LOW)
            for g in range(GROUPS):
                whole_ref[base + GROUPS + g] = d_ref[index, g * share : (g + 1) * share]
            rows = [ref[index : index + 1].astype(FULL) for ref in ins[:-1]]
            for g in range(GROUPS):
                rows.append(ins[-1][index : index + 1, g * share : (g + 1) * share].astype(FULL))
            rows.append(jnp.zeros((PAD - len(rows), share), FULL))
            packs.append(jnp.concatenate(rows, axis=0).T.astype(LOW))

        def write(target, side):
            for j, ref in enumerate((k_ref, v_ref, q_ref, o_ref)):
                target[:, j * HALF : (j + 1) * HALF] = ref[0, :, side * HALF : (side + 1) * HALF]
            target[:, 4 * HALF :] = packs[side]

        @pl.when(core_ref[0] == 0)
        def _():
            write(mine_ref, 0)
            write(sent_ref, 1)

        @pl.when(core_ref[0] != 0)
        def _():
            write(mine_ref, 1)
            write(sent_ref, 0)

    spec = pl.BlockSpec(memory_space=pltpu.VMEM)
    half = jax.ShapeDtypeStruct((share, 4 * HALF + PAD), LOW)
    return pl.pallas_call(
        kernel,
        in_specs=[pl.BlockSpec(memory_space=pltpu.SMEM)] + [spec] * (7 + len(names)),
        out_shape=[half, half, jax.ShapeDtypeStruct((4 + 4 * GROUPS, share, D), LOW)],
    )(core, *weights, moves, *[vectors[name] for name in names])


def join_rows(core, mine, other, cuts):
    def kernel(core_ref, mine_ref, other_ref, *outs):
        for (start, size), out in zip(cuts, outs):
            out[core_ref[0]] = mine_ref[:, start : start + size]
            out[1 - core_ref[0]] = other_ref[:, start : start + size]

    spec = pl.BlockSpec(memory_space=pltpu.VMEM)
    return pl.pallas_call(
        kernel,
        in_specs=[pl.BlockSpec(memory_space=pltpu.SMEM), spec, spec],
        out_shape=[jax.ShapeDtypeStruct((2, mine.shape[0], size), LOW) for _, size in cuts],
    )(core, mine, other)


def unpack_shards(core, first, second, moves):
    share = second.shape[0]

    def kernel(core_ref, second_ref, moves_ref, *refs):
        group, outs = refs[:4], refs[4:]
        grouped = second_ref[:, :FF]
        for q, part in enumerate(group_columns(grouped, moves_ref[...], back=True)):
            outs[4][1, :, q * D : (q + 1) * D] = part
        for g in range(GROUPS):
            start = (GROUPS + g) * D
            outs[5][1, g * share : (g + 1) * share] = second_ref[:, start : start + D].astype(FULL)

        def write(flipped):
            for side in range(2):
                rows = group[side ^ flipped]
                downs = group[2 + (side ^ flipped)]
                cut = slice(side * HALF, (side + 1) * HALF)
                tail = 4 * HALF + FF // 2
                for j, place in enumerate((0, 3, 1, 2)):
                    outs[place][0, :, cut] = rows[:, j * HALF : (j + 1) * HALF].astype(FULL)
                    start = tail + PAD + j * HALF
                    outs[place][1, :, cut] = rows[:, start : start + HALF].astype(FULL)
                outs[6][side] = rows[:, tail : tail + PAD].astype(FULL).T
                for g in range(GROUPS):
                    place = slice(g * share, (g + 1) * share)
                    outs[5][0, place, cut] = downs[place].astype(FULL)
            ups = [group[side ^ flipped][:, 4 * HALF : 4 * HALF + FF // 2] for side in range(2)]
            ups = group_columns(jnp.concatenate(ups, axis=1), moves_ref[...], back=True)
            for q, part in enumerate(ups):
                outs[4][0, :, q * D : (q + 1) * D] = part

        @pl.when(core_ref[0] == 0)
        def _():
            write(0)

        @pl.when(core_ref[0] != 0)
        def _():
            write(1)

    spec = pl.BlockSpec(memory_space=pltpu.VMEM)
    shapes = [(share, D)] * 4 + [(share, FF), (GROUPS * share, D), (PAD, share)]
    *weights, rows = pl.pallas_call(
        kernel,
        in_specs=[pl.BlockSpec(memory_space=pltpu.SMEM)] + [spec] * (2 + len(first)),
        out_shape=[jax.ShapeDtypeStruct((LAYERS,) + shape, FULL) for shape in shapes],
    )(core, second, moves, *first)
    vectors = {name: rows[:, i] for i, name in enumerate(NAMES[:-1])}
    vectors["up_bias"] = rows[:, 8 : 8 + GROUPS].reshape(LAYERS, -1)
    return weights, vectors


def products(normed, activated, up, down):
    rows = normed.shape[0]
    steps = 2 * GROUPS

    def kernel(normed_ref, act_ref, up_ref, down_ref, out):
        step = pl.program_id(0)

        @pl.when(step < GROUPS)
        def _():
            out[...] = dot_l(normed_ref[...], up_ref[...]).astype(LOW)

        @pl.when(step >= GROUPS)
        def _():
            out[...] = dot_l(act_ref[...], down_ref[...]).astype(LOW)

    def at(low):
        return pl.BlockSpec((rows, D), lambda i: (0, jnp.clip(i - low, 0, GROUPS - 1)))

    whole = pl.BlockSpec((rows, D), lambda i: (0, 0))
    return pl.pallas_call(
        kernel,
        grid=(steps,),
        in_specs=[whole, at(GROUPS), at(0), whole],
        out_specs=pl.BlockSpec((D, D), lambda i: (0, i)),
        out_shape=jax.ShapeDtypeStruct((D, steps * D), LOW),
        cost_estimate=pl.CostEstimate(
            flops=2 * rows * D * D * steps, bytes_accessed=D * D * steps * 2, transcendentals=0
        ),
    )(normed, activated, up, down)


def body(
    tokens,
    query_weight,
    key_weight,
    value_weight,
    out_weight,
    up_weight,
    down_weight,
    query_bias,
    value_bias,
    out_bias,
    up_bias,
    down_bias,
    first_gain,
    first_shift,
    second_gain,
    second_shift,
    lengths,
    cotangent,
):
    pairs, rows_pair, width = tokens.shape
    given = dict(
        query_bias=query_bias,
        value_bias=value_bias,
        out_bias=out_bias,
        up_bias=up_bias,
        down_bias=down_bias,
        first_gain=first_gain,
        first_shift=first_shift,
        second_gain=second_gain,
        second_shift=second_shift,
    )
    core = own_bit("narrow", 0).astype(jnp.int32).reshape(1)
    side_x = own_bit("narrow", 1)
    moves = regroup()
    mine, sent, shard = pack_shards(
        core,
        (query_weight, key_weight, value_weight, out_weight, up_weight, down_weight),
        given,
        moves,
    )
    other = swap_core(sent)
    whole = lax.all_gather(shard, ("wide", "narrow"), axis=1, tiled=True)
    kv_0, qo_0 = join_rows(core, mine, other, [(0, D), (D, D + PAD)])
    pump = Pump()
    pump.now = 13.0
    gathers = [Gather(kv_0, "wide", 0), Gather(qo_0, "narrow", 0)]
    for stream in gathers:
        pump.add(stream)

    def collect(values, rank):
        keep = lax.dynamic_index_in_dim(values, side_x, 0, keepdims=False)
        sent = lax.dynamic_index_in_dim(values, 1 - side_x, 0, keepdims=False)
        stream = Exchange(sent, 1, rank)
        pump.add(stream)

        def joined():
            pump.need([stream])
            return jnp.concatenate([keep, stream.other], axis=0)

        return joined

    def hand_back(values, rank):
        mine = values[:rows_pair]
        stream = Exchange(values[rows_pair:], 1, rank)
        pump.add(stream)
        first = side_x == 0
        return stream, lambda: jnp.stack(
            [jnp.where(first, mine, stream.other), jnp.where(first, stream.other, mine)], axis=0
        )

    narrow = lax.axis_index("narrow")
    scalars = [lax.dynamic_index_in_dim(lengths, side_x, 0, keepdims=False)]
    scalars += [(narrow ^ j) * rows_pair for j in (0, 2, 1, 3)]
    meta = jnp.stack([value.astype(jnp.int32) for value in scalars])

    hidden = collect(tokens, -1)
    upstream = collect(cotangent, 9)
    pump.need(gathers)
    parts = [(stream.mine, stream.other, 2, HALF) for stream in gathers]
    kv, qo = unfold(parts[:1]), unfold(parts[1:])
    first_pieces = dict(key=kv[:, :D], value=kv[:, D:], query=qo[:, :D], out=qo[:, D:])
    second_pieces = dict(key=whole[0], value=whole[1], query=whole[2], out=whole[3])
    layers = []
    for index, pieces in enumerate((first_pieces, second_pieces)):
        base = 4 + index * 2 * GROUPS
        pieces["up"] = [whole[base + g] for g in range(GROUPS)]
        down = whole[base + GROUPS : base + 2 * GROUPS]
        pieces["down"] = [down[g] for g in range(GROUPS)]
        pieces["down_all"] = down.reshape(FF, D)
        layers.append(pieces)
    vectors = unpack_whole(core, gathers[1].mine[:, D:], gathers[1].other[:, D:])
    kept = []
    hidden = hidden().astype(FULL)
    for index in range(LAYERS):
        hidden, saved = forward_layer(
            pump, hidden, layers[index], vectors[index], meta
        )
        kept.append(saved)
    output = hand_back(hidden.astype(LOW), 9)
    grads = [None] * LAYERS
    scatters = [None] * LAYERS

    def pack_all(first_grads):
        low, high = pack_whole(first_grads), pack_whole(grads[1])
        first = core_low()
        return jnp.where(first, low, high), jnp.where(first, high, low)

    upstream = upstream().astype(FULL)

    def hold(value):
        value, scatters[1]["ff"] = lax.optimization_barrier((value, scatters[1]["ff"]))
        return value

    for index in reversed(range(LAYERS)):
        upstream, scatters[index], grads[index] = backward_layer(
            pump,
            upstream,
            kept[index],
            layers[index],
            vectors[index],
            pack_all if index == 0 else None,
            0 if index == 1 else 4,
            hold if index == 0 else lambda value: value,
        )
    tokens_grad = hand_back(upstream.astype(LOW), 9)
    second_ff = scatters[1].pop("ff")
    for streams in scatters[::-1]:
        pump.need(streams.values())
    streams = scatters[0]
    rows = [streams[name].result[0] for name in ("qo", "kv", "up")]
    rows = [rows[0][:, :D], rows[1], rows[2], rows[0][:, D:]]
    rows += [scatters[1][name].result[0] for name in ("qo", "kv")]
    rows = jnp.concatenate(rows, axis=1)
    ends = []
    downs = streams["down"].result
    share = downs.shape[1] // 2
    downs = downs.reshape(GROUPS, 2, share, HALF).transpose(1, 0, 2, 3)
    for values in (rows, downs):
        split = values.reshape(2, -1, values.shape[-1])
        mine = lax.dynamic_index_in_dim(split, core[0], 0, keepdims=False)
        sent = lax.dynamic_index_in_dim(split, 1 - core[0], 0, keepdims=False)
        ends += [mine, swap_core(sent)]
    weight_grads, small = unpack_shards(core, ends, second_ff, moves)
    pump.need([output[0], tokens_grad[0]])
    names = (
        "query_bias",
        "value_bias",
        "out_bias",
        "up_bias",
        "down_bias",
        "first_gain",
        "first_shift",
        "second_gain",
        "second_shift",
    )
    return (output[1](), tokens_grad[1](), *weight_grads, *[small[name] for name in names])


def solution(mesh):
    rows = P("wide", "narrow", None)
    weight = P(None, ("wide", "narrow"), None)
    vector = P(None, ("wide", "narrow"))
    return jax.shard_map(
        body,
        mesh=mesh,
        in_specs=(rows,) + (weight,) * 6 + (vector,) * 9 + (P("wide"), rows),
        out_specs=(rows, rows) + (weight,) * 6 + (vector,) * 9,
        check_vma=False,
    )
```
